128 devices in a mesh: rep: 2 (over x_hi), row: 8 (over y, core), col: 8 (over x_lo, z).
Axes of the slice: x: 4 (x_hi: 2, x_lo: 2; x = x_hi * 2 + x_lo), y: 4, z: 4, core: 2. Of those that a mesh axis runs over, the one named last changes fastest.
Arguments:
- replica_deltas: bfloat16 [2, 4096, 4096], P('rep', 'row', 'col'), may hold values from -8 to 8
- weights: float32 [4096, 4096], P('row', 'col'), may hold values from -6 to 6
- momentum: float32 [4096, 4096], P('row', 'col'), may hold values from -6 to 6
- left_state: float32 [4096, 4096], P('row', ('rep', 'col')), may hold values from -0.5 to 4.5
- right_state: float32 [4096, 4096], P(('rep', 'row'), 'col'), may hold values from -0.5 to 4.5
- left_root: bfloat16 [4096, 4096], P('row', ('rep', 'col')), may hold values from -0.5 to 2.5
- right_root: bfloat16 [4096, 4096], P(('rep', 'row'), 'col'), may hold values from -0.5 to 2.5
Outputs:
- new_weights: float32 [4096, 4096], P('row', 'col')
- new_momentum: float32 [4096, 4096], P('row', 'col')
- new_left: float32 [4096, 4096], P('row', ('rep', 'col'))
- new_right: float32 [4096, 4096], P(('rep', 'row'), 'col')
The draws below stay inside these ranges and needn't reach their ends.
All inputs are finite; a program needn't handle non-finite values.
Results may differ from the reference program's by a relative error of at most 0.0054.
Values may be sent and summed in bfloat16 or wider, within the bound.
A program may use at most 128 MiB of HBM per device.

```python
import math
import jax
import jax.numpy as jnp
from jax import lax

ROWS = 4096
COLS = 4096
N_REP = 2


def assemble(noise, diagonal, scale):
    order = noise.shape[0]
    first = lax_iota(order)[:, None]
    second = lax_iota(order)[None, :]
    return jnp.where(first == second, diagonal[:, None], 0.0) + noise * scale


def lax_iota(order):
    return jnp.arange(order, dtype=jnp.int32)


def draw_left_state(key, part):
    key = jax.random.fold_in(key, 3)
    noise_key, diag_key = jax.random.split(key)
    noise = jax.random.normal(noise_key, (ROWS, ROWS), jnp.float32)
    diagonal = jax.random.uniform(diag_key, (ROWS,), jnp.float32, 0.5, 2.0)
    return assemble(noise, diagonal, 0.5 / math.sqrt(ROWS))


def draw_right_state(key, part):
    key = jax.random.fold_in(key, 5)
    noise_key, diag_key = jax.random.split(key)
    noise = jax.random.normal(noise_key, (COLS, COLS), jnp.float32)
    diagonal = jax.random.uniform(diag_key, (COLS,), jnp.float32, 0.5, 2.0)
    return assemble(noise, diagonal, 0.5 / math.sqrt(COLS))


def draw_left_root(key, part):
    key = jax.random.fold_in(key, 7)
    noise_key, diag_key = jax.random.split(key)
    noise = jax.random.normal(noise_key, (ROWS, ROWS), jnp.float32)
    diagonal = jax.random.uniform(diag_key, (ROWS,), jnp.float32, 0.5, 1.5)
    return assemble(noise, diagonal, 0.5 / math.sqrt(ROWS)).astype(jnp.bfloat16)


def draw_right_root(key, part):
    key = jax.random.fold_in(key, 9)
    noise_key, diag_key = jax.random.split(key)
    noise = jax.random.normal(noise_key, (COLS, COLS), jnp.float32)
    diagonal = jax.random.uniform(diag_key, (COLS,), jnp.float32, 0.5, 1.5)
    return assemble(noise, diagonal, 0.5 / math.sqrt(COLS)).astype(jnp.bfloat16)


def level_of(stream_key, shape, cuts, smallest, high):
    loudness, own = 1.0, jax.random.fold_in(stream_key, 6)
    for dim, parts in cuts:
        draws = jnp.exp(jax.random.uniform(jax.random.fold_in(own, dim), (parts,), jnp.float32, smallest / len(cuts), high / len(cuts)))
        loudness = loudness * jnp.repeat(draws, shape[dim] // parts).reshape([-1 if axis == dim else 1 for axis in range(len(shape))])
    return loudness


def bell_draw(rng, dims, spread, limit, cuts=(), kind=jnp.bfloat16):
    factor_of = level_of(rng, dims, cuts, -0.22, 0.18) if cuts else 1.0
    array = jax.random.normal(rng, dims, jnp.float32) * spread * factor_of
    return jnp.minimum(jnp.maximum(array, -limit), limit).astype(kind)


def setup_inputs(seed: int = 0) -> dict:
    streams_of = jax.random.split(jax.random.key(seed), 8)
    return {
        "replica_deltas": bell_draw(streams_of[0], (N_REP, ROWS, COLS), 2.0, 8.0, ((0, 2), (1, 8), (2, 8))),
        "weights": bell_draw(streams_of[1], (ROWS, COLS), 1.0, 6.0, ((0, 8), (1, 8)), jnp.float32),
        "momentum": bell_draw(streams_of[2], (ROWS, COLS), 1.0, 6.0, ((0, 8), (1, 8)), jnp.float32),
        "left_state": draw_left_state(jax.random.fold_in(streams_of[7], 71), 0),
        "right_state": draw_right_state(jax.random.fold_in(streams_of[7], 71), 0),
        "left_root": draw_left_root(jax.random.fold_in(streams_of[7], 71), 0),
        "right_root": draw_right_root(jax.random.fold_in(streams_of[7], 71), 0),
    }


decay_rate = 0.9
momentum_rate = 0.9
outer_rate = 0.7


def reference(replica_deltas, weights, momentum, left_state, right_state, left_root, right_root):
    pseudo = jnp.sum(replica_deltas.astype(jnp.float32), axis=0) / N_REP
    grad = pseudo.astype(jnp.bfloat16)
    left_gram = lax.dot_general(grad, grad, (((1,), (1,)), ((), ())), preferred_element_type=jnp.float32)
    right_gram = lax.dot_general(grad, grad, (((0,), (0,)), ((), ())), preferred_element_type=jnp.float32)
    new_left = decay_rate * left_state + ((1.0 - decay_rate) / COLS) * left_gram
    new_right = decay_rate * right_state + ((1.0 - decay_rate) / ROWS) * right_gram
    mixed = jnp.dot(grad, right_root, preferred_element_type=jnp.float32).astype(jnp.bfloat16)
    precond = jnp.dot(left_root, mixed, preferred_element_type=jnp.float32)
    new_momentum = momentum_rate * momentum + precond
    new_weights = weights - outer_rate * (momentum_rate * new_momentum + precond)
    return new_weights, new_momentum, new_left, new_right
```

```python
import functools

import jax
import jax.numpy as jnp
from jax import lax
from jax.experimental import pallas as pl
from jax.experimental.pallas import tpu as pltpu
from jax.sharding import PartitionSpec as P

decay_rate = 0.9
momentum_rate = 0.9
outer_rate = 0.7

MESH = pl.DeviceIdType.MESH
ORDER = (1, 3, 2)
HALF = 256
FULL = 512
SPLIT = 256
N_COPIES = 85


def lanes(chunk):
    return pl.ds(pl.multiple_of(chunk * HALF, HALF), HALF)


def rows_at(chunk, size):
    return pl.ds(pl.multiple_of(chunk * size, size), size)


def nn(a, b):
    return jnp.dot(a, b, preferred_element_type=jnp.float32)


def nt(a, b):
    return lax.dot_general(a, b, (((1,), (1,)), ((), ())), preferred_element_type=jnp.float32)


def tn(a, b):
    return lax.dot_general(a, b, (((0,), (0,)), ((), ())), preferred_element_type=jnp.float32)


def kernel(
    delta, left_root, right_root,
    out_pre, out_left, out_right,
    d_own, d_in, g_row, l_row, r_col, m_col, l_band,
    q_out, q_own, q_in, s_out, s_in, p_out, p_in,
    local_sem, send_sem, recv_sem,
):
    rep = lax.axis_index("rep")
    row = lax.axis_index("row")
    col = lax.axis_index("col")
    x, y, z, h = rep * 2 + col // 4, row // 2, col % 4, row % 2
    xl = col // 4

    def dev(xx, yy, zz, hh):
        return (xx // 2, yy * 2 + hh, (xx % 2) * 4 + zz)

    def along_x(d):
        return dev((x + d) % 4, y, z, h)

    def along_y(d):
        return dev(x, (y + d) % 4, z, h)

    def along_z(d):
        return dev(x, y, (z + d) % 4, h)

    mate = dev(x, y, z, 1 - h)
    twin = along_x(2)
    turned = [dev(y, x, 2 * h + i, 1 - z // 2) for i in range(2)]
    turned_from = [dev(y, x, 2 * (1 - h) + i, z // 2) for i in range(2)]

    copies = []

    def send(src, dst, device, slot=None):
        i = len(copies)
        cp = pltpu.make_async_remote_copy(
            src_ref=src, dst_ref=dst, send_sem=send_sem.at[i],
            recv_sem=recv_sem.at[i if slot is None else slot],
            device_id=device, device_id_type=MESH,
        )
        cp.start()
        copies.append(cp)
        return cp

    own_g = lanes(4 * z + x)
    own_l = lanes(4 * x + z)
    own_r = rows_at(4 * y + 2 * h + rep, HALF)
    load_l = pltpu.make_async_copy(left_root, l_row.at[:, own_l], local_sem.at[0])
    load_d = pltpu.make_async_copy(delta.at[:, lanes(rep)], d_own, local_sem.at[1])
    load_r = pltpu.make_async_copy(right_root.at[:, lanes(rep)], r_col.at[own_r], local_sem.at[2])
    load_d.start()
    load_l.start()
    load_r.start()

    barrier = pltpu.get_barrier_semaphore()
    partners = [f(d) for f in (along_x, along_y, along_z) for d in ORDER] + [mate] + turned + turned_from
    for partner in partners:
        pl.semaphore_signal(barrier, inc=1, device_id=partner, device_id_type=MESH)
    pl.semaphore_wait(barrier, len(partners))

    d_swap = send(delta.at[:, lanes(1 - rep)], d_in, twin)
    r_swap = send(right_root.at[:, lanes(1 - rep)], r_col.at[own_r], twin)

    load_l.wait()
    l_z = {d: send(l_row.at[:, own_l], l_row.at[:, own_l], along_z(d)) for d in ORDER}

    load_d.wait()
    d_swap.wait_recv()
    g_row[:, own_g] = (
        (d_own[...].astype(jnp.float32) + d_in[...].astype(jnp.float32)) * 0.5
    ).astype(jnp.bfloat16)

    g_z = {d: send(g_row.at[:, own_g], g_row.at[:, own_g], along_z(d)) for d in ORDER}
    g_x = {d: send(g_row.at[:, own_g], g_row.at[:, own_g], along_x(d)) for d in ORDER}
    slot = len(copies)
    turn = [
        send(g_row.at[pl.ds(HALF * i, HALF), own_g], l_band.at[:, own_g], turned[i], slot + z % 2)
        for i in range(2)
    ]

    def y_sends(refs):
        to_y = {d: [send(r, r, along_y(d)) for r in refs] for d in ORDER}
        return to_y, [send(r, r, mate) for r in refs]

    def y_forwards(to_y, refs_of):
        out = []
        for d in ORDER:
            for cp in to_y[d]:
                cp.wait_recv()
            out += [send(r, r, mate) for r in refs_of((y + 4 - d) % 4)]
        return out

    def r_refs(yy):
        return [r_col.at[rows_at(2 * yy + h, FULL)]]

    def b_refs(yy):
        return [l_band.at[:, lanes(4 * (2 * (1 - h) + i) + yy)] for i in range(2)]

    def m_refs(yy):
        return [m_col.at[rows_at(2 * yy + h, FULL)]]

    load_r.wait()
    r_swap.wait_recv()
    r_y, r_mate = y_sends(r_refs(y))

    rows_a, rows_b = pl.ds(0, SPLIT), pl.ds(SPLIT, FULL - SPLIT)

    def forward_a(buf, chunk):
        ref = buf.at[rows_a, lanes(chunk)]
        return [send(ref, ref, along_x(d)) for d in ORDER]

    def forward_b(buf, chunk):
        ref = buf.at[rows_b, lanes(chunk)]
        return [send(ref, ref, along_z(d)) for d in ORDER]

    g_last = []
    for n, d in enumerate(ORDER):
        g_z[d].wait_recv()
        g_last += forward_a(g_row, 4 * ((z + 4 - d) % 4) + x)
        g_x[d].wait_recv()
        g_last += forward_b(g_row, 4 * z + (x + 4 - d) % 4)
        if n == 0:
            for i in range(2):
                pltpu.make_async_copy(l_band.at[:, own_g], l_band.at[:, own_g], recv_sem.at[slot + i]).wait()
            b_y, b_mate = y_sends(b_refs(y))
    r_mate += y_forwards(r_y, r_refs)
    l_x = {d: send(l_row.at[:, own_l], l_row.at[:, own_l], along_x(d)) for d in ORDER}
    b_mate += y_forwards(b_y, b_refs)
    for cp in g_last:
        cp.wait_recv()
    l_last = []
    for d in ORDER:
        l_z[d].wait_recv()
        l_last += forward_a(l_row, 4 * x + (z + 4 - d) % 4)

    for cp in r_mate:
        cp.wait_recv()
    base = (2 * y + h) * FULL

    @pl.loop(0, 2)
    def _(i):
        tile = nn(g_row[pl.ds(pl.multiple_of(i * HALF, HALF), HALF), :], r_col[...])
        m_col[pl.ds(pl.multiple_of(base + i * HALF, HALF), HALF), :] = tile.astype(jnp.bfloat16)

    m_y, m_mate = y_sends(m_refs(y))

    for d in ORDER:
        l_x[d].wait_recv()
        l_last += forward_b(l_row, 4 * ((x + 4 - d) % 4) + z)

    band = [lanes(4 * z + xl), lanes(4 * z + 2 + xl)]

    @pl.loop(0, 4)
    def _(yy):
        other = g_row[:, lanes(4 * yy + 2 * (1 - h) + rep)]
        for i in range(2):
            q_out[yy, :, pl.ds(HALF * i, HALF)] = tn(other, g_row[:, band[i]]).astype(jnp.bfloat16)

    q_swap = send(q_out, q_in, mate)

    @pl.loop(0, 4)
    def _(yy):
        mine = g_row[:, lanes(4 * yy + 2 * h + rep)]
        for i in range(2):
            q_own[yy, :, pl.ds(HALF * i, HALF)] = tn(mine, g_row[:, band[i]])

    q_swap.wait_recv()

    @pl.loop(0, 4)
    def _(yy):
        total = q_own[yy] + q_in[yy].astype(jnp.float32)
        q_own[yy] = total
        s_out[yy] = total.astype(jnp.bfloat16)

    s_y = [send(s_out.at[(y + d) % 4], s_in.at[n], along_y(d)) for n, d in enumerate(ORDER)]

    for cp in b_mate:
        cp.wait_recv()

    @pl.loop(0, 2)
    def _(i):
        part = pl.ds(pl.multiple_of(i * HALF, HALF), HALF)
        out_left[part, :] = nt(g_row[part, :], l_band[...])

    m_mate += y_forwards(m_y, m_refs)

    for cp in l_last:
        cp.wait_recv()
    for cp in m_mate:
        cp.wait_recv()

    @pl.loop(0, 2)
    def _(i):
        part = pl.ds(pl.multiple_of(i * HALF, HALF), HALF)
        tile = nn(l_row[part, :], m_col[...])
        out_pre[part, lanes(rep)] = tile
        p_out[part, :] = tile.astype(jnp.bfloat16)

    p_swap = send(p_out, p_in, twin)

    for cp in s_y:
        cp.wait_recv()
    out_right[...] = (
        q_own[y] + s_in[0].astype(jnp.float32) + s_in[1].astype(jnp.float32) + s_in[2].astype(jnp.float32)
    )

    p_swap.wait_recv()
    out_pre[:, lanes(1 - rep)] = p_in[...].astype(jnp.float32)

    for cp in copies:
        cp.wait_send()
    assert len(copies) == N_COPIES, len(copies)


def shards(replica_deltas, weights, momentum, left_state, right_state, left_root, right_root):
    total = left_root.shape[0] * lax.axis_size("row")
    bf16, f32 = jnp.bfloat16, jnp.float32
    any_spec = pl.BlockSpec(memory_space=pl.ANY)
    vmem_spec = pl.BlockSpec(memory_space=pltpu.VMEM)
    update, left_gram, right_gram = pl.pallas_call(
        kernel,
        name="shampoo",
        out_shape=(
            jax.ShapeDtypeStruct((FULL, FULL), f32),
            jax.ShapeDtypeStruct((FULL, HALF), f32),
            jax.ShapeDtypeStruct((HALF, FULL), f32),
        ),
        in_specs=[any_spec] * 3,
        out_specs=[vmem_spec] * 3,
        scratch_shapes=[
            pltpu.VMEM((FULL, HALF), bf16),
            pltpu.VMEM((FULL, HALF), bf16),
            pltpu.VMEM((FULL, total), bf16),
            pltpu.VMEM((FULL, total), bf16),
            pltpu.VMEM((total, HALF), bf16),
            pltpu.VMEM((total, HALF), bf16),
            pltpu.VMEM((HALF, total), bf16),
            pltpu.VMEM((4, HALF, FULL), bf16),
            pltpu.VMEM((4, HALF, FULL), f32),
            pltpu.VMEM((4, HALF, FULL), bf16),
            pltpu.VMEM((4, HALF, FULL), bf16),
            pltpu.VMEM((3, HALF, FULL), bf16),
            pltpu.VMEM((FULL, HALF), bf16),
            pltpu.VMEM((FULL, HALF), bf16),
            pltpu.SemaphoreType.DMA((3,)),
            pltpu.SemaphoreType.DMA((N_COPIES,)),
            pltpu.SemaphoreType.DMA((N_COPIES,)),
        ],
        compiler_params=pltpu.CompilerParams(
            collective_id=0, has_side_effects=True, vmem_limit_bytes=56 * 2**20
        ),
        cost_estimate=pl.CostEstimate(flops=8 * 2**30, bytes_accessed=4 * 2**20, transcendentals=0),
    )(replica_deltas[0], left_root, right_root)
    new_left = decay_rate * left_state + (1.0 - decay_rate) / total * left_gram
    new_right = decay_rate * right_state + (1.0 - decay_rate) / total * right_gram
    new_momentum = momentum_rate * momentum + update
    new_weights = weights - outer_rate * (momentum_rate * new_momentum + update)
    return (new_weights, new_momentum, new_left, new_right)


def solution(mesh):
    in_specs = (
        P("rep", "row", "col"),
        P("row", "col"),
        P("row", "col"),
        P("row", ("rep", "col")),
        P(("rep", "row"), "col"),
        P("row", ("rep", "col")),
        P(("rep", "row"), "col"),
    )
    out_specs = (
        P("row", "col"),
        P("row", "col"),
        P("row", ("rep", "col")),
        P(("rep", "row"), "col"),
    )
    return jax.shard_map(shards, mesh=mesh, in_specs=in_specs, out_specs=out_specs, check_vma=False)
```

```python
import functools

import jax
import jax.numpy as jnp
from jax import lax
from jax.experimental import pallas as pl
from jax.experimental.pallas import tpu as pltpu
from jax.sharding import PartitionSpec as P

decay_rate = 0.9
momentum_rate = 0.9
outer_rate = 0.7

MESH = pl.DeviceIdType.MESH
HALF = 256
FULL = 512
SPLIT = 160
N_COPIES = 105


def lanes(chunk):
    return pl.ds(pl.multiple_of(chunk * HALF, HALF), HALF)


def rows_at(chunk, size):
    return pl.ds(pl.multiple_of(chunk * size, size), size)


def nn(a, b):
    return jnp.dot(a, b, preferred_element_type=jnp.float32)


def nt(a, b):
    return lax.dot_general(a, b, (((1,), (1,)), ((), ())), preferred_element_type=jnp.float32)


def tn(a, b):
    return lax.dot_general(a, b, (((0,), (0,)), ((), ())), preferred_element_type=jnp.float32)


def kernel(
    delta, left_root, right_root,
    out_pre, out_left, out_right,
    d_own, d_in, g_row, l_row, r_col, m_col, l_band,
    q_out, q_own, q_in, s_out, s_in, p_out, p_in,
    local_sem, send_sem, recv_sem,
):
    rep = lax.axis_index("rep")
    row = lax.axis_index("row")
    col = lax.axis_index("col")
    x, y, z, h = rep * 2 + col // 4, row // 2, col % 4, row % 2
    xl = col // 4

    def dev(xx, yy, zz, hh):
        return (xx // 2, yy * 2 + hh, (xx % 2) * 4 + zz)

    def along_x(d):
        return dev((x + 4 + d) % 4, y, z, h)

    def along_y(d):
        return dev(x, (y + 4 + d) % 4, z, h)

    def along_z(d):
        return dev(x, y, (z + 4 + d) % 4, h)

    mate = dev(x, y, z, 1 - h)
    twin = along_x(2)
    turned = [dev(y, x, 2 * h + i, 1 - z // 2) for i in range(2)]
    turned_from = [dev(y, x, 2 * (1 - h) + i, z // 2) for i in range(2)]

    copies = []

    def send(src, dst, device, slot=None):
        i = len(copies)
        cp = pltpu.make_async_remote_copy(
            src_ref=src, dst_ref=dst, send_sem=send_sem.at[i],
            recv_sem=recv_sem.at[i if slot is None else slot],
            device_id=device, device_id_type=MESH,
        )
        cp.start()
        copies.append(cp)
        return cp

    class Ring:
        def __init__(self, along, at, refs, sign=1, share=False):
            self.along, self.at, self.refs, self.sign, self.share = along, at, refs, sign, share
            self.shared = []
            self.first = {d: self.push(at, None, d) for d in (1, -1)}
            self.second = {}
            self.give(at, None)

        def push(self, i, part, d):
            return [send(r, r, self.along(d)) for r in self.refs(i, part)]

        def give(self, i, part):
            if self.share:
                self.shared += [send(r, r, mate) for r in self.refs(i, part)]

        def turn(self, d):
            for cp in self.first[d]:
                cp.wait_recv()
            i = (self.at + 4 - d) % 4
            self.second[d] = self.push(i, 0 if d == self.sign else 1, d)
            self.give(i, None)

        def end(self, d):
            for cp in self.second[d]:
                cp.wait_recv()
            self.give((self.at + 2) % 4, 0 if d == self.sign else 1)

        def got(self):
            for cp in self.shared:
                cp.wait_recv()

    class Plane:
        def __init__(self, buf, spot, sign):
            self.buf, self.spot, self.sign = buf, spot, sign
            self.rings = []

        def rows(self, lo, hi, xx, zz):
            return [self.buf.at[pl.ds(lo, hi - lo), lanes(self.spot(xx, zz))]]

        def start_z(self):
            cuts = {None: (0, FULL), 0: (0, SPLIT), 1: (SPLIT, FULL)}
            self.z = Ring(along_z, z, lambda i, part: self.rows(*cuts[part], x, i), self.sign)

        def start_x(self):
            cuts = {None: (0, FULL), 0: (SPLIT, FULL), 1: (0, SPLIT)}
            self.x = Ring(along_x, x, lambda i, part: self.rows(*cuts[part], i, z), self.sign)

        def on_x(self, zz):
            cuts = {None: (0, SPLIT), 0: (0, SPLIT // 2), 1: (SPLIT // 2, SPLIT)}
            self.rings.append(Ring(along_x, x, lambda i, part: self.rows(*cuts[part], i, zz), self.sign))

        def on_z(self, xx):
            mid = (SPLIT + FULL) // 2
            cuts = {None: (SPLIT, FULL), 0: (SPLIT, mid), 1: (mid, FULL)}
            self.rings.append(Ring(along_z, z, lambda i, part: self.rows(*cuts[part], xx, i), self.sign))

        def turn_z(self, d):
            self.z.turn(d)
            self.on_x((z + 4 - d) % 4)

        def turn_x(self, d):
            self.x.turn(d)
            self.on_z((x + 4 - d) % 4)

        def far_z(self):
            self.z.end(self.sign)
            self.on_x((z + 2) % 4)

        def far_x(self):
            self.x.end(self.sign)
            self.on_z((x + 2) % 4)

        def turn_rings(self):
            for ring in self.rings:
                ring.turn(1)
                ring.turn(-1)

        def end(self):
            self.z.end(-self.sign)
            self.x.end(-self.sign)
            for ring in self.rings:
                ring.end(1)
                ring.end(-1)

    own_g = lanes(4 * z + x)
    own_l = lanes(4 * x + z)
    own_r = rows_at(4 * y + 2 * h + rep, HALF)
    load_l = pltpu.make_async_copy(left_root, l_row.at[:, own_l], local_sem.at[0])
    load_d = pltpu.make_async_copy(delta.at[:, lanes(rep)], d_own, local_sem.at[1])
    load_r = pltpu.make_async_copy(right_root.at[:, lanes(rep)], r_col.at[own_r], local_sem.at[2])
    load_d.start()
    load_l.start()
    load_r.start()

    barrier = pltpu.get_barrier_semaphore()
    partners = [f(d) for f in (along_x, along_y, along_z) for d in (1, -1)]
    partners += [twin, mate, along_y(2)] + turned + turned_from
    for partner in partners:
        pl.semaphore_signal(barrier, inc=1, device_id=partner, device_id_type=MESH)
    pl.semaphore_wait(barrier, len(partners))

    d_swap = send(delta.at[:, lanes(1 - rep)], d_in, twin)
    load_l.wait()
    left = Plane(l_row, lambda xx, zz: 4 * xx + zz, -1)
    left.start_z()

    load_d.wait()
    d_swap.wait_recv()
    g_row[:, own_g] = (
        (d_own[...].astype(jnp.float32) + d_in[...].astype(jnp.float32)) * 0.5
    ).astype(jnp.bfloat16)

    grad = Plane(g_row, lambda xx, zz: 4 * zz + xx, 1)
    grad.start_x()
    grad.start_z()
    slot = len(copies)
    turn = [
        send(g_row.at[pl.ds(HALF * i, HALF), own_g], l_band.at[:, own_g], turned[i], slot + z % 2)
        for i in range(2)
    ]
    r_swap = send(right_root.at[:, lanes(1 - rep)], r_col.at[own_r], twin)
    left.z.turn(1)
    left.z.turn(-1)

    def pair(buf):
        def refs(yy, part):
            base, size = (2 * yy + h) * FULL, FULL
            if part is not None:
                base, size = base + part * HALF, HALF
            return [buf.at[pl.ds(pl.multiple_of(base, HALF), size)]]

        return refs

    def band_refs(yy, part):
        return [
            l_band.at[:, lanes(4 * (2 * (1 - h) + i) + yy)]
            for i in ((0, 1) if part is None else (part,))
        ]

    grad.turn_x(1)
    grad.turn_z(1)
    grad.turn_x(-1)
    grad.turn_z(-1)
    load_r.wait()
    r_swap.wait_recv()
    r_ring = Ring(along_y, y, pair(r_col), share=True)
    grad.far_x()
    grad.far_z()
    for i in range(2):
        pltpu.make_async_copy(l_band.at[:, own_g], l_band.at[:, own_g], recv_sem.at[slot + i]).wait()
    b_ring = Ring(along_y, y, band_refs, share=True)
    grad.turn_rings()
    left.start_x()
    for ring in (r_ring, b_ring):
        ring.turn(1)
        ring.turn(-1)
    grad.end()
    left.on_x((z + 3) % 4)
    left.on_x((z + 1) % 4)
    left.far_z()
    for ring in (r_ring, b_ring):
        ring.end(1)
        ring.end(-1)
    r_ring.got()

    base = (2 * y + h) * FULL

    @pl.loop(0, 2)
    def _(i):
        tile = nn(g_row[pl.ds(pl.multiple_of(i * HALF, HALF), HALF), :], r_col[...])
        m_col[pl.ds(pl.multiple_of(base + i * HALF, HALF), HALF), :] = tile.astype(jnp.bfloat16)

    m_ring = Ring(along_y, y, pair(m_col), share=True)

    left.turn_x(1)
    left.turn_x(-1)

    band = [lanes(4 * z + xl), lanes(4 * z + 2 + xl)]

    @pl.loop(0, 4)
    def _(yy):
        other = g_row[:, lanes(4 * yy + 2 * (1 - h) + rep)]
        for i in range(2):
            q_out[yy, :, pl.ds(HALF * i, HALF)] = tn(other, g_row[:, band[i]]).astype(jnp.bfloat16)

    q_swap = send(q_out, q_in, mate)
    left.far_x()
    left.turn_rings()
    m_ring.turn(1)
    m_ring.turn(-1)

    @pl.loop(0, 4)
    def _(yy):
        mine = g_row[:, lanes(4 * yy + 2 * h + rep)]
        for i in range(2):
            q_own[yy, :, pl.ds(HALF * i, HALF)] = tn(mine, g_row[:, band[i]])

    q_swap.wait_recv()

    @pl.loop(0, 4)
    def _(yy):
        total = q_own[yy] + q_in[yy].astype(jnp.float32)
        q_own[yy] = total
        s_out[yy] = total.astype(jnp.bfloat16)

    s_y = [send(s_out.at[(y + 4 + d) % 4], s_in.at[n], along_y(d)) for n, d in enumerate((1, -1, 2))]
    m_ring.end(1)
    m_ring.end(-1)

    b_ring.got()

    @pl.loop(0, 2)
    def _(i):
        part = pl.ds(pl.multiple_of(i * HALF, HALF), HALF)
        out_left[part, :] = nt(g_row[part, :], l_band[...])

    left.end()
    m_ring.got()

    @pl.loop(0, 2)
    def _(i):
        part = pl.ds(pl.multiple_of(i * HALF, HALF), HALF)
        tile = nn(l_row[part, :], m_col[...])
        out_pre[part, lanes(rep)] = tile
        p_out[part, :] = tile.astype(jnp.bfloat16)

    p_swap = send(p_out, p_in, twin)

    for cp in s_y:
        cp.wait_recv()
    out_right[...] = (
        q_own[y] + s_in[0].astype(jnp.float32) + s_in[1].astype(jnp.float32) + s_in[2].astype(jnp.float32)
    )

    p_swap.wait_recv()
    out_pre[:, lanes(1 - rep)] = p_in[...].astype(jnp.float32)

    for cp in copies:
        cp.wait_send()
    assert len(copies) == N_COPIES, len(copies)


def shards(replica_deltas, weights, momentum, left_state, right_state, left_root, right_root):
    total = left_root.shape[0] * lax.axis_size("row")
    bf16, f32 = jnp.bfloat16, jnp.float32
    any_spec = pl.BlockSpec(memory_space=pl.ANY)
    vmem_spec = pl.BlockSpec(memory_space=pltpu.VMEM)
    update, left_gram, right_gram = pl.pallas_call(
        kernel,
        name="shampoo",
        out_shape=(
            jax.ShapeDtypeStruct((FULL, FULL), f32),
            jax.ShapeDtypeStruct((FULL, HALF), f32),
            jax.ShapeDtypeStruct((HALF, FULL), f32),
        ),
        in_specs=[any_spec] * 3,
        out_specs=[vmem_spec] * 3,
        scratch_shapes=[
            pltpu.VMEM((FULL, HALF), bf16),
            pltpu.VMEM((FULL, HALF), bf16),
            pltpu.VMEM((FULL, total), bf16),
            pltpu.VMEM((FULL, total), bf16),
            pltpu.VMEM((total, HALF), bf16),
            pltpu.VMEM((total, HALF), bf16),
            pltpu.VMEM((HALF, total), bf16),
            pltpu.VMEM((4, HALF, FULL), bf16),
            pltpu.VMEM((4, HALF, FULL), f32),
            pltpu.VMEM((4, HALF, FULL), bf16),
            pltpu.VMEM((4, HALF, FULL), bf16),
            pltpu.VMEM((3, HALF, FULL), bf16),
            pltpu.VMEM((FULL, HALF), bf16),
            pltpu.VMEM((FULL, HALF), bf16),
            pltpu.SemaphoreType.DMA((3,)),
            pltpu.SemaphoreType.DMA((N_COPIES,)),
            pltpu.SemaphoreType.DMA((N_COPIES,)),
        ],
        compiler_params=pltpu.CompilerParams(
            collective_id=0, has_side_effects=True, vmem_limit_bytes=56 * 2**20
        ),
        cost_estimate=pl.CostEstimate(flops=8 * 2**30, bytes_accessed=4 * 2**20, transcendentals=0),
    )(replica_deltas[0], left_root, right_root)
    new_left = decay_rate * left_state + (1.0 - decay_rate) / total * left_gram
    new_right = decay_rate * right_state + (1.0 - decay_rate) / total * right_gram
    new_momentum = momentum_rate * momentum + update
    new_weights = weights - outer_rate * (momentum_rate * new_momentum + update)
    return (new_weights, new_momentum, new_left, new_right)


def solution(mesh):
    in_specs = (
        P("rep", "row", "col"),
        P("row", "col"),
        P("row", "col"),
        P("row", ("rep", "col")),
        P(("rep", "row"), "col"),
        P("row", ("rep", "col")),
        P(("rep", "row"), "col"),
    )
    out_specs = (
        P("row", "col"),
        P("row", "col"),
        P("row", ("rep", "col")),
        P(("rep", "row"), "col"),
    )
    return jax.shard_map(shards, mesh=mesh, in_specs=in_specs, out_specs=out_specs, check_vma=False)
```

```python
import functools

import jax
import jax.numpy as jnp
from jax import lax
from jax.experimental import pallas as pl
from jax.experimental.pallas import tpu as pltpu
from jax.sharding import PartitionSpec as P

decay_rate = 0.9
momentum_rate = 0.9
outer_rate = 0.7

MESH = pl.DeviceIdType.MESH
HALF = 256
FULL = 512
QUARTER = 64
SPLIT = 224
N_COPIES = 131


def lanes(chunk):
    return pl.ds(pl.multiple_of(chunk * HALF, HALF), HALF)


def rows_at(chunk, size):
    return pl.ds(pl.multiple_of(chunk * size, size), size)


def nn(a, b):
    return jnp.dot(a, b, preferred_element_type=jnp.float32)


def nt(a, b):
    return lax.dot_general(a, b, (((1,), (1,)), ((), ())), preferred_element_type=jnp.float32)


def tn(a, b):
    return lax.dot_general(a, b, (((0,), (0,)), ((), ())), preferred_element_type=jnp.float32)


def kernel(
    delta, left_root, right_root,
    out_pre, out_left, out_right,
    d_own, d_in, g_row, l_row, r_col, m_col, l_band,
    b_part, q_out, q_own, q_in, s_out, s_in, p_out, p_in,
    local_sem, send_sem, recv_sem,
):
    rep = lax.axis_index("rep")
    row = lax.axis_index("row")
    col = lax.axis_index("col")
    x, y, z, h = rep * 2 + col // 4, row // 2, col % 4, row % 2
    xl = col // 4

    def dev(xx, yy, zz, hh):
        return (xx // 2, yy * 2 + hh, (xx % 2) * 4 + zz)

    def along_x(d):
        return dev((x + 4 + d) % 4, y, z, h)

    def along_y(d):
        return dev(x, (y + 4 + d) % 4, z, h)

    def along_z(d):
        return dev(x, y, (z + 4 + d) % 4, h)

    mate = dev(x, y, z, 1 - h)
    twin = along_x(2)
    turned = [[dev((y + 4 - d) % 4, y, 2 * h + i, 1 - z // 2) for i in range(2)] for d in range(4)]
    turned_from = [dev(xx, y, 2 * (1 - h) + i, z // 2) for xx in range(4) for i in range(2)]

    copies = []

    def send(src, dst, device, slot=None):
        i = len(copies)
        cp = pltpu.make_async_remote_copy(
            src_ref=src, dst_ref=dst, send_sem=send_sem.at[i],
            recv_sem=recv_sem.at[i if slot is None else slot],
            device_id=device, device_id_type=MESH,
        )
        cp.start()
        copies.append(cp)
        return cp

    class Ring:
        def __init__(self, along, at, refs, onward, share=False):
            self.along, self.at, self.refs, self.onward, self.share = along, at, refs, onward, share
            self.shared = []
            self.first = {d: self.push(at, None, d) for d in (1, -1)}
            self.second = {}
            self.give(at, None)

        def push(self, i, part, d):
            return [send(r, r, self.along(d)) for r in self.refs(i, part)]

        def give(self, i, part):
            if self.share:
                self.shared += [send(r, r, mate) for r in self.refs(i, part)]

        def turn(self, d):
            for cp in self.first[d]:
                cp.wait_recv()
            i = (self.at + 4 - d) % 4
            if d in self.onward:
                self.second[d] = self.push(i, self.onward[d], d)
            self.give(i, None)

        def end(self, d):
            for cp in self.second[d]:
                cp.wait_recv()
            self.give((self.at + 2) % 4, self.onward[d])

        def got(self):
            for cp in self.shared:
                cp.wait_recv()

    halves = {1: 0, -1: 1}
    spans = ((0, SPLIT), (SPLIT, FULL))

    class Plane:
        def __init__(self, buf, spot, sign):
            self.buf, self.spot, self.sign = buf, spot, sign
            self.rings, self.z, self.x = [], [None, None], [None, None]

        def rows(self, span, part, xx, zz):
            lo, hi = span
            mid = (lo + hi) // 2
            lo, hi = {None: (lo, hi), 0: (lo, mid), 1: (mid, hi)}[part]
            return [self.buf.at[pl.ds(lo, hi - lo), lanes(self.spot(xx, zz))]]

        def start_z(self, k):
            refs = lambda i, part: self.rows(spans[k], part, x, i)
            self.z[k] = Ring(along_z, z, refs, {self.sign if k == 0 else -self.sign: None})

        def start_x(self, k):
            refs = lambda i, part: self.rows(spans[k], part, i, z)
            self.x[k] = Ring(along_x, x, refs, {self.sign if k == 1 else -self.sign: None})

        def on_x(self, zz):
            refs = lambda i, part: self.rows(spans[0], part, i, zz)
            self.rings.append(Ring(along_x, x, refs, halves))

        def on_z(self, xx):
            refs = lambda i, part: self.rows(spans[1], part, xx, i)
            self.rings.append(Ring(along_z, z, refs, halves))

        def turn_z(self, k):
            for d in (self.sign, -self.sign):
                self.z[k].turn(d)

        def turn_x(self, k):
            for d in (self.sign, -self.sign):
                self.x[k].turn(d)

        def near_z(self):
            self.on_x((z + 4 - self.sign) % 4)
            self.on_x((z + 4 + self.sign) % 4)

        def near_x(self):
            self.on_z((x + 4 - self.sign) % 4)
            self.on_z((x + 4 + self.sign) % 4)

        def far_z(self):
            self.z[0].end(self.sign)
            self.on_x((z + 2) % 4)

        def far_x(self):
            self.x[1].end(self.sign)
            self.on_z((x + 2) % 4)

        def turn_rings(self):
            for ring in self.rings:
                ring.turn(1)
                ring.turn(-1)

        def end(self):
            self.z[1].end(-self.sign)
            self.x[0].end(-self.sign)
            for ring in self.rings:
                ring.end(1)
                ring.end(-1)

    own_g = lanes(4 * z + x)
    own_l = lanes(4 * x + z)
    own_r = rows_at(4 * y + 2 * h + rep, HALF)
    load_l = pltpu.make_async_copy(left_root, l_row.at[:, own_l], local_sem.at[0])
    load_d = pltpu.make_async_copy(delta.at[:, lanes(rep)], d_own, local_sem.at[1])
    load_r = pltpu.make_async_copy(right_root.at[:, lanes(rep)], r_col.at[own_r], local_sem.at[2])
    load_d.start()
    load_l.start()
    load_r.start()

    barrier = pltpu.get_barrier_semaphore()
    partners = [f(d) for f in (along_x, along_y, along_z) for d in (1, -1)]
    partners += [twin, mate, along_y(2)] + sum(turned, []) + turned_from
    for partner in partners:
        pl.semaphore_signal(barrier, inc=1, device_id=partner, device_id_type=MESH)
    pl.semaphore_wait(barrier, len(partners))

    d_swap = []
    for lo, hi in spans:
        part = pl.ds(lo, hi - lo)
        d_swap.append(send(delta.at[part, lanes(1 - rep)], d_in.at[part, :], twin))
    load_l.wait()
    left = Plane(l_row, lambda xx, zz: 4 * xx + zz, -1)
    left.start_z(0)
    left.start_z(1)

    load_d.wait()
    grad = Plane(g_row, lambda xx, zz: 4 * zz + xx, 1)
    for k, (lo, hi) in enumerate(spans):
        part = pl.ds(lo, hi - lo)
        d_swap[k].wait_recv()
        g_row[part, own_g] = (
            (d_own[part, :].astype(jnp.float32) + d_in[part, :].astype(jnp.float32)) * 0.5
        ).astype(jnp.bfloat16)
        grad.start_z(k)
        grad.start_x(k)
    spread = {
        d: [
            send(
                g_row.at[pl.ds(pl.multiple_of(HALF * i + QUARTER * ((y + d) % 4), QUARTER), QUARTER), own_g],
                b_part.at[d - 1, i], along_y(d),
            )
            for i in range(2)
        ]
        for d in (1, 3, 2)
    }
    r_swap = send(right_root.at[:, lanes(1 - rep)], r_col.at[own_r], twin)
    left.turn_z(0)
    left.turn_z(1)

    def pair(buf):
        def refs(yy, part):
            base, size = (2 * yy + h) * FULL, FULL
            if part is not None:
                base, size = base + part * HALF, HALF
            return [buf.at[pl.ds(pl.multiple_of(base, HALF), size)]]

        return refs

    side = pl.ds(pl.multiple_of((1 - h) * 8 * HALF, HALF), 8 * HALF)

    def band_refs(yy, part):
        lo, size = QUARTER * yy, QUARTER
        if part is not None:
            lo, size = lo + part * (QUARTER // 2), QUARTER // 2
        return [l_band.at[pl.ds(pl.multiple_of(lo, QUARTER // 2), size), side]]

    grad.turn_z(0)
    grad.near_z()
    grad.turn_x(0)
    turn = []
    slot = len(copies)
    own_q = pl.ds(pl.multiple_of(QUARTER * y, QUARTER), QUARTER)
    for d in (0, 1, 3, 2):
        for i in range(2):
            if d == 0:
                src = g_row.at[pl.ds(pl.multiple_of(HALF * i + QUARTER * y, QUARTER), QUARTER), own_g]
            else:
                spread[d][i].wait_recv()
                src = b_part.at[d - 1, i]
            turn.append(send(src, l_band.at[own_q, own_g], turned[d][i], slot + 2 * x + z % 2))
    grad.turn_z(1)
    grad.turn_x(1)
    grad.near_x()
    load_r.wait()
    r_swap.wait_recv()
    r_ring = Ring(along_y, y, pair(r_col), halves, share=True)
    grad.far_z()
    grad.far_x()
    for i in range(8):
        pltpu.make_async_copy(
            l_band.at[own_q, own_g], l_band.at[own_q, own_g], recv_sem.at[slot + i]
        ).wait()
    b_ring = Ring(along_y, y, band_refs, halves, share=True)
    grad.turn_rings()
    left.start_x(1)
    left.start_x(0)
    for ring in (r_ring, b_ring):
        ring.turn(1)
        ring.turn(-1)
    grad.end()
    left.near_z()
    left.far_z()
    for ring in (r_ring, b_ring):
        ring.end(1)
        ring.end(-1)
    r_ring.got()

    base = (2 * y + h) * FULL

    def m_part(k):
        def refs(yy, part):
            lo, size = (2 * yy + h) * FULL + k * HALF, HALF
            if part is not None:
                lo, size = lo + part * (HALF // 2), HALF // 2
            return [m_col.at[pl.ds(pl.multiple_of(lo, HALF // 2), size)]]

        return refs

    m_rings = []
    for k in range(2):
        tile = nn(g_row[pl.ds(k * HALF, HALF), :], r_col[...])
        m_col[pl.ds(pl.multiple_of(base + k * HALF, HALF), HALF), :] = tile.astype(jnp.bfloat16)
        m_rings.append(Ring(along_y, y, m_part(k), halves, share=True))

    left.turn_x(1)
    left.near_x()
    left.turn_x(0)

    band = [lanes(4 * z + xl), lanes(4 * z + 2 + xl)]

    @pl.loop(0, 4)
    def _(yy):
        other = g_row[:, lanes(4 * yy + 2 * (1 - h) + rep)]
        for i in range(2):
            q_out[yy, :, pl.ds(HALF * i, HALF)] = tn(other, g_row[:, band[i]]).astype(jnp.bfloat16)

    q_swap = send(q_out, q_in, mate)
    left.far_x()
    left.turn_rings()
    for ring in m_rings:
        ring.turn(1)
        ring.turn(-1)

    @pl.loop(0, 4)
    def _(yy):
        mine = g_row[:, lanes(4 * yy + 2 * h + rep)]
        for i in range(2):
            q_own[yy, :, pl.ds(HALF * i, HALF)] = tn(mine, g_row[:, band[i]])

    q_swap.wait_recv()

    @pl.loop(0, 4)
    def _(yy):
        total = q_own[yy] + q_in[yy].astype(jnp.float32)
        q_own[yy] = total
        s_out[yy] = total.astype(jnp.bfloat16)

    s_y = [send(s_out.at[(y + 4 + d) % 4], s_in.at[n], along_y(d)) for n, d in enumerate((1, -1, 2))]
    for ring in m_rings:
        ring.end(1)
        ring.end(-1)

    b_ring.got()

    @pl.loop(0, 2)
    def _(i):
        part = pl.ds(pl.multiple_of(i * HALF, HALF), HALF)
        out_left[part, :] = nt(g_row[part, :], l_band[...])

    left.end()
    for ring in m_rings:
        ring.got()

    p_swap = []
    for k in range(2):
        part = pl.ds(k * HALF, HALF)
        tile = nn(l_row[part, :], m_col[...])
        p_out[part, :] = tile.astype(jnp.bfloat16)
        p_swap.append(send(p_out.at[part, :], p_in.at[part, :], twin))
        out_pre[part, lanes(rep)] = tile

    for cp in s_y:
        cp.wait_recv()
    out_right[...] = (
        q_own[y] + s_in[0].astype(jnp.float32) + s_in[1].astype(jnp.float32) + s_in[2].astype(jnp.float32)
    )

    for k in range(2):
        part = pl.ds(k * HALF, HALF)
        p_swap[k].wait_recv()
        out_pre[part, lanes(1 - rep)] = p_in[part, :].astype(jnp.float32)

    for cp in copies:
        cp.wait_send()
    assert len(copies) == N_COPIES, len(copies)


def shards(replica_deltas, weights, momentum, left_state, right_state, left_root, right_root):
    total = left_root.shape[0] * lax.axis_size("row")
    bf16, f32 = jnp.bfloat16, jnp.float32
    any_spec = pl.BlockSpec(memory_space=pl.ANY)
    vmem_spec = pl.BlockSpec(memory_space=pltpu.VMEM)
    update, left_gram, right_gram = pl.pallas_call(
        kernel,
        name="shampoo",
        out_shape=(
            jax.ShapeDtypeStruct((FULL, FULL), f32),
            jax.ShapeDtypeStruct((FULL, HALF), f32),
            jax.ShapeDtypeStruct((HALF, FULL), f32),
        ),
        in_specs=[any_spec] * 3,
        out_specs=[vmem_spec] * 3,
        scratch_shapes=[
            pltpu.VMEM((FULL, HALF), bf16),
            pltpu.VMEM((FULL, HALF), bf16),
            pltpu.VMEM((FULL, total), bf16),
            pltpu.VMEM((FULL, total), bf16),
            pltpu.VMEM((total, HALF), bf16),
            pltpu.VMEM((total, HALF), bf16),
            pltpu.VMEM((HALF, total), bf16),
            pltpu.VMEM((3, 2, QUARTER, HALF), bf16),
            pltpu.VMEM((4, HALF, FULL), bf16),
            pltpu.VMEM((4, HALF, FULL), f32),
            pltpu.VMEM((4, HALF, FULL), bf16),
            pltpu.VMEM((4, HALF, FULL), bf16),
            pltpu.VMEM((3, HALF, FULL), bf16),
            pltpu.VMEM((FULL, HALF), bf16),
            pltpu.VMEM((FULL, HALF), bf16),
            pltpu.SemaphoreType.DMA((3,)),
            pltpu.SemaphoreType.DMA((N_COPIES,)),
            pltpu.SemaphoreType.DMA((N_COPIES,)),
        ],
        compiler_params=pltpu.CompilerParams(
            collective_id=0, has_side_effects=True, vmem_limit_bytes=56 * 2**20
        ),
        cost_estimate=pl.CostEstimate(flops=8 * 2**30, bytes_accessed=4 * 2**20, transcendentals=0),
    )(replica_deltas[0], left_root, right_root)
    new_left = decay_rate * left_state + (1.0 - decay_rate) / total * left_gram
    new_right = decay_rate * right_state + (1.0 - decay_rate) / total * right_gram
    new_momentum = momentum_rate * momentum + update
    new_weights = weights - outer_rate * (momentum_rate * new_momentum + update)
    return (new_weights, new_momentum, new_left, new_right)


def solution(mesh):
    in_specs = (
        P("rep", "row", "col"),
        P("row", "col"),
        P("row", "col"),
        P("row", ("rep", "col")),
        P(("rep", "row"), "col"),
        P("row", ("rep", "col")),
        P(("rep", "row"), "col"),
    )
    out_specs = (
        P("row", "col"),
        P("row", "col"),
        P("row", ("rep", "col")),
        P(("rep", "row"), "col"),
    )
    return jax.shard_map(shards, mesh=mesh, in_specs=in_specs, out_specs=out_specs, check_vma=False)
```

```python
import functools

import jax
import jax.numpy as jnp
from jax import lax
from jax.experimental import pallas as pl
from jax.experimental.pallas import tpu as pltpu
from jax.sharding import PartitionSpec as P

decay_rate = 0.9
momentum_rate = 0.9
outer_rate = 0.7

MESH = pl.DeviceIdType.MESH
HALF = 256
FULL = 512
QUARTER = 64
SPLIT = 224
N_COPIES = 131


def lanes(chunk):
    return pl.ds(pl.multiple_of(chunk * HALF, HALF), HALF)


def rows_at(chunk, size):
    return pl.ds(pl.multiple_of(chunk * size, size), size)


def nn(a, b):
    return jnp.dot(a, b, preferred_element_type=jnp.float32)


def nt(a, b):
    return lax.dot_general(a, b, (((1,), (1,)), ((), ())), preferred_element_type=jnp.float32)


def tn(a, b):
    return lax.dot_general(a, b, (((0,), (0,)), ((), ())), preferred_element_type=jnp.float32)


def kernel(
    delta, left_root, right_root, left_state, right_state,
    out_pre, out_left, out_right,
    d_own, d_in, g_row, l_row, r_col, m_col, l_band,
    b_part, q_out, q_own, q_in, s_out, s_in, p_out, p_in, state_l, state_r,
    local_sem, send_sem, recv_sem,
):
    rep = lax.axis_index("rep")
    row = lax.axis_index("row")
    col = lax.axis_index("col")
    x, y, z, h = rep * 2 + col // 4, row // 2, col % 4, row % 2
    xl = col // 4

    def dev(xx, yy, zz, hh):
        return (xx // 2, yy * 2 + hh, (xx % 2) * 4 + zz)

    def along_x(d):
        return dev((x + 4 + d) % 4, y, z, h)

    def along_y(d):
        return dev(x, (y + 4 + d) % 4, z, h)

    def along_z(d):
        return dev(x, y, (z + 4 + d) % 4, h)

    mate = dev(x, y, z, 1 - h)
    twin = along_x(2)
    turned = [[dev((y + 4 - d) % 4, y, 2 * h + i, 1 - z // 2) for i in range(2)] for d in range(4)]
    turned_from = [dev(xx, y, 2 * (1 - h) + i, z // 2) for xx in range(4) for i in range(2)]

    copies = []

    def send(src, dst, device, slot=None):
        i = len(copies)
        cp = pltpu.make_async_remote_copy(
            src_ref=src, dst_ref=dst, send_sem=send_sem.at[i],
            recv_sem=recv_sem.at[i if slot is None else slot],
            device_id=device, device_id_type=MESH,
        )
        cp.start()
        copies.append(cp)
        return cp

    class Ring:
        def __init__(self, along, at, refs, onward, share=False):
            self.along, self.at, self.refs, self.onward, self.share = along, at, refs, onward, share
            self.shared = []
            self.first = {d: self.push(at, None, d) for d in (1, -1)}
            self.second = {}
            self.give(at, None)

        def push(self, i, part, d):
            return [send(r, r, self.along(d)) for r in self.refs(i, part)]

        def give(self, i, part):
            if self.share:
                self.shared += [send(r, r, mate) for r in self.refs(i, part)]

        def turn(self, d):
            for cp in self.first[d]:
                cp.wait_recv()
            i = (self.at + 4 - d) % 4
            if d in self.onward:
                self.second[d] = self.push(i, self.onward[d], d)
            self.give(i, None)

        def end(self, d):
            for cp in self.second[d]:
                cp.wait_recv()
            self.give((self.at + 2) % 4, self.onward[d])

        def got(self):
            for cp in self.shared:
                cp.wait_recv()

    halves = {1: 0, -1: 1}
    spans = ((0, SPLIT), (SPLIT, FULL))

    class Plane:
        def __init__(self, buf, spot, sign):
            self.buf, self.spot, self.sign = buf, spot, sign
            self.rings, self.z, self.x = [], [None, None], [None, None]

        def rows(self, span, part, xx, zz):
            lo, hi = span
            mid = (lo + hi) // 2
            lo, hi = {None: (lo, hi), 0: (lo, mid), 1: (mid, hi)}[part]
            return [self.buf.at[pl.ds(lo, hi - lo), lanes(self.spot(xx, zz))]]

        def start_z(self, k):
            refs = lambda i, part: self.rows(spans[k], part, x, i)
            self.z[k] = Ring(along_z, z, refs, {self.sign if k == 0 else -self.sign: None})

        def start_x(self, k):
            refs = lambda i, part: self.rows(spans[k], part, i, z)
            self.x[k] = Ring(along_x, x, refs, {self.sign if k == 1 else -self.sign: None})

        def on_x(self, zz):
            refs = lambda i, part: self.rows(spans[0], part, i, zz)
            self.rings.append(Ring(along_x, x, refs, halves))

        def on_z(self, xx):
            refs = lambda i, part: self.rows(spans[1], part, xx, i)
            self.rings.append(Ring(along_z, z, refs, halves))

        def turn_z(self, k):
            for d in (self.sign, -self.sign):
                self.z[k].turn(d)

        def turn_x(self, k):
            for d in (self.sign, -self.sign):
                self.x[k].turn(d)

        def near_z(self):
            self.on_x((z + 4 - self.sign) % 4)
            self.on_x((z + 4 + self.sign) % 4)

        def near_x(self):
            self.on_z((x + 4 - self.sign) % 4)
            self.on_z((x + 4 + self.sign) % 4)

        def far_z(self):
            self.z[0].end(self.sign)
            self.on_x((z + 2) % 4)

        def far_x(self):
            self.x[1].end(self.sign)
            self.on_z((x + 2) % 4)

        def turn_rings(self):
            for ring in self.rings:
                ring.turn(1)
                ring.turn(-1)

        def end(self, k):
            (self.x, self.z)[k][k].end(-self.sign)
            for ring in self.rings:
                if ring.along is (along_x, along_z)[k]:
                    ring.end(1)
                    ring.end(-1)

    own_g = lanes(4 * z + x)
    own_l = lanes(4 * x + z)
    own_r = rows_at(4 * y + 2 * h + rep, HALF)
    load_l = pltpu.make_async_copy(left_root, l_row.at[:, own_l], local_sem.at[0])
    load_d = pltpu.make_async_copy(delta.at[:, lanes(rep)], d_own, local_sem.at[1])
    load_r = pltpu.make_async_copy(right_root.at[:, lanes(rep)], r_col.at[own_r], local_sem.at[2])
    load_d.start()
    load_l.start()
    load_r.start()
    load_sl = pltpu.make_async_copy(left_state, state_l, local_sem.at[3])
    load_sr = pltpu.make_async_copy(right_state, state_r, local_sem.at[4])

    barrier = pltpu.get_barrier_semaphore()
    partners = [f(d) for f in (along_x, along_y, along_z) for d in (1, -1)]
    partners += [twin, mate, along_y(2)] + sum(turned, []) + turned_from
    for partner in partners:
        pl.semaphore_signal(barrier, inc=1, device_id=partner, device_id_type=MESH)
    pl.semaphore_wait(barrier, len(partners))

    d_swap = []
    for lo, hi in spans:
        part = pl.ds(lo, hi - lo)
        d_swap.append(send(delta.at[part, lanes(1 - rep)], d_in.at[part, :], twin))
    load_l.wait()
    left = Plane(l_row, lambda xx, zz: 4 * xx + zz, -1)
    left.start_z(0)
    left.start_z(1)

    load_d.wait()
    grad = Plane(g_row, lambda xx, zz: 4 * zz + xx, 1)
    for k, (lo, hi) in enumerate(spans):
        part = pl.ds(lo, hi - lo)
        d_swap[k].wait_recv()
        g_row[part, own_g] = (
            (d_own[part, :].astype(jnp.float32) + d_in[part, :].astype(jnp.float32)) * 0.5
        ).astype(jnp.bfloat16)
        grad.start_z(k)
        grad.start_x(k)
    spread = {
        d: [
            send(
                g_row.at[pl.ds(pl.multiple_of(HALF * i + QUARTER * ((y + d) % 4), QUARTER), QUARTER), own_g],
                b_part.at[d - 1, i], along_y(d),
            )
            for i in range(2)
        ]
        for d in (1, 3, 2)
    }
    r_swap = send(right_root.at[:, lanes(1 - rep)], r_col.at[own_r], twin)
    left.turn_z(0)
    left.turn_z(1)

    def pair(buf):
        def refs(yy, part):
            base, size = (2 * yy + h) * FULL, FULL
            if part is not None:
                base, size = base + part * HALF, HALF
            return [buf.at[pl.ds(pl.multiple_of(base, HALF), size)]]

        return refs

    side = pl.ds(pl.multiple_of((1 - h) * 8 * HALF, HALF), 8 * HALF)

    def band_refs(yy, part):
        lo, size = QUARTER * yy, QUARTER
        if part is not None:
            lo, size = lo + part * (QUARTER // 2), QUARTER // 2
        return [l_band.at[pl.ds(pl.multiple_of(lo, QUARTER // 2), size), side]]

    grad.turn_z(0)
    grad.near_z()
    grad.turn_x(0)
    turn = []
    slot = len(copies)
    own_q = pl.ds(pl.multiple_of(QUARTER * y, QUARTER), QUARTER)
    for d in (0, 1, 3, 2):
        for i in range(2):
            if d == 0:
                src = g_row.at[pl.ds(pl.multiple_of(HALF * i + QUARTER * y, QUARTER), QUARTER), own_g]
            else:
                spread[d][i].wait_recv()
                src = b_part.at[d - 1, i]
            turn.append(send(src, l_band.at[own_q, own_g], turned[d][i], slot + 2 * x + z % 2))
    grad.turn_z(1)
    grad.turn_x(1)
    grad.near_x()
    load_r.wait()
    load_sl.start()
    load_sr.start()
    r_swap.wait_recv()
    r_ring = Ring(along_y, y, pair(r_col), halves, share=True)
    grad.far_z()
    grad.far_x()
    for i in range(8):
        pltpu.make_async_copy(
            l_band.at[own_q, own_g], l_band.at[own_q, own_g], recv_sem.at[slot + i]
        ).wait()
    b_ring = Ring(along_y, y, band_refs, halves, share=True)
    grad.turn_rings()
    left.start_x(1)
    left.start_x(0)
    for ring in (r_ring, b_ring):
        ring.turn(1)
        ring.turn(-1)
    left.near_z()
    left.far_z()
    for ring in (r_ring, b_ring):
        ring.end(1)
        ring.end(-1)
    r_ring.got()

    base = (2 * y + h) * FULL

    def m_part(k):
        def refs(yy, part):
            lo, hi = spans[k]
            mid = (lo + hi) // 2
            lo, hi = {None: (lo, hi), 0: (lo, mid), 1: (mid, hi)}[part]
            return [m_col.at[pl.ds(pl.multiple_of((2 * yy + h) * FULL + lo, 16), hi - lo)]]

        return refs

    m_rings = []
    for k, (lo, hi) in enumerate(spans):
        grad.end(k)
        tile = nn(g_row[pl.ds(lo, hi - lo), :], r_col[...])
        m_col[pl.ds(pl.multiple_of(base + lo, 16), hi - lo), :] = tile.astype(jnp.bfloat16)
        m_rings.append(Ring(along_y, y, m_part(k), halves, share=True))

    left.turn_x(1)
    left.near_x()
    left.turn_x(0)

    band = [lanes(4 * z + xl), lanes(4 * z + 2 + xl)]

    @pl.loop(0, 4)
    def _(yy):
        other = g_row[:, lanes(4 * yy + 2 * (1 - h) + rep)]
        for i in range(2):
            q_out[yy, :, pl.ds(HALF * i, HALF)] = tn(other, g_row[:, band[i]]).astype(jnp.bfloat16)

    q_swap = send(q_out, q_in, mate)
    left.far_x()
    left.turn_rings()
    for ring in m_rings:
        ring.turn(1)
        ring.turn(-1)

    @pl.loop(0, 4)
    def _(yy):
        mine = g_row[:, lanes(4 * yy + 2 * h + rep)]
        for i in range(2):
            q_own[yy, :, pl.ds(HALF * i, HALF)] = tn(mine, g_row[:, band[i]])

    q_swap.wait_recv()

    @pl.loop(0, 4)
    def _(yy):
        total = q_own[yy] + q_in[yy].astype(jnp.float32)
        q_own[yy] = total
        s_out[yy] = total.astype(jnp.bfloat16)

    s_y = [send(s_out.at[(y + 4 + d) % 4], s_in.at[n], along_y(d)) for n, d in enumerate((1, -1, 2))]
    for ring in m_rings:
        ring.end(1)
        ring.end(-1)

    gain = (1.0 - decay_rate) / g_row.shape[1]
    load_sl.wait()
    load_sr.wait()
    b_ring.got()

    @pl.loop(0, 2)
    def _(i):
        part = pl.ds(pl.multiple_of(i * HALF, HALF), HALF)
        out_left[part, :] = decay_rate * state_l[part, :] + gain * nt(g_row[part, :], l_band[...])

    for ring in m_rings:
        ring.got()
    p_swap = []
    for k, (lo, hi) in enumerate(spans):
        part = pl.ds(lo, hi - lo)
        left.end(k)
        tile = nn(l_row[part, :], m_col[...])
        p_out[part, :] = tile.astype(jnp.bfloat16)
        p_swap.append(send(p_out.at[part, :], p_in.at[part, :], twin))
        out_pre[part, lanes(rep)] = tile

    for cp in s_y:
        cp.wait_recv()
    out_right[...] = decay_rate * state_r[...] + gain * (
        q_own[y] + s_in[0].astype(jnp.float32) + s_in[1].astype(jnp.float32) + s_in[2].astype(jnp.float32)
    )

    for k, (lo, hi) in enumerate(spans):
        part = pl.ds(lo, hi - lo)
        p_swap[k].wait_recv()
        out_pre[part, lanes(1 - rep)] = p_in[part, :].astype(jnp.float32)
    for cp in copies:
        cp.wait_send()
    assert len(copies) == N_COPIES, len(copies)


def shards(replica_deltas, weights, momentum, left_state, right_state, left_root, right_root):
    total = left_root.shape[0] * lax.axis_size("row")
    bf16, f32 = jnp.bfloat16, jnp.float32
    any_spec = pl.BlockSpec(memory_space=pl.ANY)
    vmem_spec = pl.BlockSpec(memory_space=pltpu.VMEM)
    update, new_left, new_right = pl.pallas_call(
        kernel,
        name="shampoo",
        out_shape=(
            jax.ShapeDtypeStruct((FULL, FULL), f32),
            jax.ShapeDtypeStruct((FULL, HALF), f32),
            jax.ShapeDtypeStruct((HALF, FULL), f32),
        ),
        in_specs=[any_spec] * 5,
        out_specs=[vmem_spec] * 3,
        scratch_shapes=[
            pltpu.VMEM((FULL, HALF), bf16),
            pltpu.VMEM((FULL, HALF), bf16),
            pltpu.VMEM((FULL, total), bf16),
            pltpu.VMEM((FULL, total), bf16),
            pltpu.VMEM((total, HALF), bf16),
            pltpu.VMEM((total, HALF), bf16),
            pltpu.VMEM((HALF, total), bf16),
            pltpu.VMEM((3, 2, QUARTER, HALF), bf16),
            pltpu.VMEM((4, HALF, FULL), bf16),
            pltpu.VMEM((4, HALF, FULL), f32),
            pltpu.VMEM((4, HALF, FULL), bf16),
            pltpu.VMEM((4, HALF, FULL), bf16),
            pltpu.VMEM((3, HALF, FULL), bf16),
            pltpu.VMEM((FULL, HALF), bf16),
            pltpu.VMEM((FULL, HALF), bf16),
            pltpu.VMEM((FULL, HALF), f32),
            pltpu.VMEM((HALF, FULL), f32),
            pltpu.SemaphoreType.DMA((5,)),
            pltpu.SemaphoreType.DMA((N_COPIES,)),
            pltpu.SemaphoreType.DMA((N_COPIES,)),
        ],
        compiler_params=pltpu.CompilerParams(
            collective_id=0, has_side_effects=True, vmem_limit_bytes=56 * 2**20
        ),
        cost_estimate=pl.CostEstimate(flops=8 * 2**30, bytes_accessed=4 * 2**20, transcendentals=0),
    )(replica_deltas[0], left_root, right_root, left_state, right_state)
    new_momentum = momentum_rate * momentum + update
    new_weights = weights - outer_rate * (momentum_rate * new_momentum + update)
    return (new_weights, new_momentum, new_left, new_right)


def solution(mesh):
    in_specs = (
        P("rep", "row", "col"),
        P("row", "col"),
        P("row", "col"),
        P("row", ("rep", "col")),
        P(("rep", "row"), "col"),
        P("row", ("rep", "col")),
        P(("rep", "row"), "col"),
    )
    out_specs = (
        P("row", "col"),
        P("row", "col"),
        P("row", ("rep", "col")),
        P(("rep", "row"), "col"),
    )
    return jax.shard_map(shards, mesh=mesh, in_specs=in_specs, out_specs=out_specs, check_vma=False)
```

```python
import functools

import jax
import jax.numpy as jnp
from jax import lax
from jax.experimental import pallas as pl
from jax.experimental.pallas import tpu as pltpu
from jax.sharding import PartitionSpec as P

decay_rate = 0.9
momentum_rate = 0.9
outer_rate = 0.7

MESH = pl.DeviceIdType.MESH
HALF = 256
FULL = 512
QUARTER = 64
SPLIT = 224
N_COPIES = 131


def lanes(chunk):
    return pl.ds(pl.multiple_of(chunk * HALF, HALF), HALF)


def rows_at(chunk, size):
    return pl.ds(pl.multiple_of(chunk * size, size), size)


def nn(a, b):
    return jnp.dot(a, b, preferred_element_type=jnp.float32)


def nt(a, b):
    return lax.dot_general(a, b, (((1,), (1,)), ((), ())), preferred_element_type=jnp.float32)


def tn(a, b):
    return lax.dot_general(a, b, (((0,), (0,)), ((), ())), preferred_element_type=jnp.float32)


def kernel(
    delta, left_root, right_root, left_state, right_state,
    out_pre, out_left, out_right,
    d_own, d_in, g_row, l_row, r_col, m_col, l_band,
    b_part, q_out, q_own, q_in, s_out, s_in, p_out, p_in, state_l, state_r,
    local_sem, send_sem, recv_sem,
):
    rep = lax.axis_index("rep")
    row = lax.axis_index("row")
    col = lax.axis_index("col")
    x, y, z, h = rep * 2 + col // 4, row // 2, col % 4, row % 2
    xl = col // 4

    def dev(xx, yy, zz, hh):
        return (xx // 2, yy * 2 + hh, (xx % 2) * 4 + zz)

    def along_x(d):
        return dev((x + 4 + d) % 4, y, z, h)

    def along_y(d):
        return dev(x, (y + 4 + d) % 4, z, h)

    def along_z(d):
        return dev(x, y, (z + 4 + d) % 4, h)

    mate = dev(x, y, z, 1 - h)
    twin = along_x(2)
    turned = [[dev((y + 4 - d) % 4, y, 2 * h + i, 1 - z // 2) for i in range(2)] for d in range(4)]
    turned_from = [dev(xx, y, 2 * (1 - h) + i, z // 2) for xx in range(4) for i in range(2)]

    copies = []

    def send(src, dst, device, slot=None):
        i = len(copies)
        cp = pltpu.make_async_remote_copy(
            src_ref=src, dst_ref=dst, send_sem=send_sem.at[i],
            recv_sem=recv_sem.at[i if slot is None else slot],
            device_id=device, device_id_type=MESH,
        )
        cp.start()
        copies.append(cp)
        return cp

    class Ring:
        def __init__(self, along, at, refs, onward, share=False):
            self.along, self.at, self.refs, self.onward, self.share = along, at, refs, onward, share
            self.shared = []
            self.first = {d: self.push(at, None, d) for d in (1, -1)}
            self.second = {}
            self.give(at, None)

        def push(self, i, part, d):
            return [send(r, r, self.along(d)) for r in self.refs(i, part)]

        def give(self, i, part):
            if self.share:
                self.shared += [send(r, r, mate) for r in self.refs(i, part)]

        def turn(self, d):
            for cp in self.first[d]:
                cp.wait_recv()
            i = (self.at + 4 - d) % 4
            if d in self.onward:
                self.second[d] = self.push(i, self.onward[d], d)
            self.give(i, None)

        def end(self, d):
            for cp in self.second[d]:
                cp.wait_recv()
            self.give((self.at + 2) % 4, self.onward[d])

        def got(self):
            for cp in self.shared:
                cp.wait_recv()

    halves = {1: 0, -1: 1}
    spans = ((0, SPLIT), (SPLIT, FULL))

    class Plane:
        def __init__(self, buf, spot, sign):
            self.buf, self.spot, self.sign = buf, spot, sign
            self.rings, self.z, self.x = [], [None, None], [None, None]

        def rows(self, span, part, xx, zz):
            lo, hi = span
            mid = (lo + hi) // 2
            lo, hi = {None: (lo, hi), 0: (lo, mid), 1: (mid, hi)}[part]
            return [self.buf.at[pl.ds(lo, hi - lo), lanes(self.spot(xx, zz))]]

        def start_z(self, k):
            refs = lambda i, part: self.rows(spans[k], part, x, i)
            self.z[k] = Ring(along_z, z, refs, {self.sign if k == 0 else -self.sign: None})

        def start_x(self, k):
            refs = lambda i, part: self.rows(spans[k], part, i, z)
            self.x[k] = Ring(along_x, x, refs, {self.sign if k == 1 else -self.sign: None})

        def on_x(self, zz):
            refs = lambda i, part: self.rows(spans[0], part, i, zz)
            self.rings.append(Ring(along_x, x, refs, halves))

        def on_z(self, xx):
            refs = lambda i, part: self.rows(spans[1], part, xx, i)
            self.rings.append(Ring(along_z, z, refs, halves))

        def turn_z(self, k):
            for d in (self.sign, -self.sign):
                self.z[k].turn(d)

        def turn_x(self, k):
            for d in (self.sign, -self.sign):
                self.x[k].turn(d)

        def near_z(self):
            self.on_x((z + 4 - self.sign) % 4)
            self.on_x((z + 4 + self.sign) % 4)

        def near_x(self):
            self.on_z((x + 4 - self.sign) % 4)
            self.on_z((x + 4 + self.sign) % 4)

        def far_z(self):
            self.z[0].end(self.sign)
            self.on_x((z + 2) % 4)

        def far_x(self):
            self.x[1].end(self.sign)
            self.on_z((x + 2) % 4)

        def turn_rings(self):
            for ring in self.rings:
                ring.turn(1)
                ring.turn(-1)

        def end(self, k):
            (self.x, self.z)[k][k].end(-self.sign)
            for ring in self.rings:
                if ring.along is (along_x, along_z)[k]:
                    ring.end(1)
                    ring.end(-1)

    own_g = lanes(4 * z + x)
    own_l = lanes(4 * x + z)
    own_r = rows_at(4 * y + 2 * h + rep, HALF)
    load_l = pltpu.make_async_copy(left_root, l_row.at[:, own_l], local_sem.at[0])
    load_d = pltpu.make_async_copy(delta.at[:, lanes(rep)], d_own, local_sem.at[1])
    load_r = pltpu.make_async_copy(right_root.at[:, lanes(rep)], r_col.at[own_r], local_sem.at[2])
    load_d.start()
    load_l.start()
    load_r.start()
    load_sl = pltpu.make_async_copy(left_state, state_l, local_sem.at[3])
    load_sr = pltpu.make_async_copy(right_state, state_r, local_sem.at[4])

    barrier = pltpu.get_barrier_semaphore()
    partners = [f(d) for f in (along_x, along_y, along_z) for d in (1, -1)]
    partners += [twin, mate, along_y(2)] + sum(turned, []) + turned_from
    for partner in partners:
        pl.semaphore_signal(barrier, inc=1, device_id=partner, device_id_type=MESH)
    pl.semaphore_wait(barrier, len(partners))

    d_swap = []
    for lo, hi in spans:
        part = pl.ds(lo, hi - lo)
        d_swap.append(send(delta.at[part, lanes(1 - rep)], d_in.at[part, :], twin))
    load_l.wait()
    left = Plane(l_row, lambda xx, zz: 4 * xx + zz, -1)
    left.start_z(0)
    left.start_z(1)

    load_d.wait()
    grad = Plane(g_row, lambda xx, zz: 4 * zz + xx, 1)
    for k, (lo, hi) in enumerate(spans):
        part = pl.ds(lo, hi - lo)
        d_swap[k].wait_recv()
        g_row[part, own_g] = (
            (d_own[part, :].astype(jnp.float32) + d_in[part, :].astype(jnp.float32)) * 0.5
        ).astype(jnp.bfloat16)
        grad.start_z(k)
        grad.start_x(k)
    spread = {
        d: [
            send(
                g_row.at[pl.ds(pl.multiple_of(HALF * i + QUARTER * ((y + d) % 4), QUARTER), QUARTER), own_g],
                b_part.at[d - 1, i], along_y(d),
            )
            for i in range(2)
        ]
        for d in (1, 3, 2)
    }
    r_swap = send(right_root.at[:, lanes(1 - rep)], r_col.at[own_r], twin)
    left.turn_z(0)
    left.turn_z(1)

    def pair(buf):
        def refs(yy, part):
            base, size = (2 * yy + h) * FULL, FULL
            if part is not None:
                base, size = base + part * HALF, HALF
            return [buf.at[pl.ds(pl.multiple_of(base, HALF), size)]]

        return refs

    side = pl.ds(pl.multiple_of((1 - h) * 8 * HALF, HALF), 8 * HALF)

    def band_refs(yy, part):
        lo, size = QUARTER * yy, QUARTER
        if part is not None:
            lo, size = lo + part * (QUARTER // 2), QUARTER // 2
        return [l_band.at[pl.ds(pl.multiple_of(lo, QUARTER // 2), size), side]]

    grad.turn_z(0)
    grad.near_z()
    grad.turn_x(0)
    turn = []
    slot = len(copies)
    own_q = pl.ds(pl.multiple_of(QUARTER * y, QUARTER), QUARTER)
    for d in (0, 1, 3, 2):
        for i in range(2):
            if d == 0:
                src = g_row.at[pl.ds(pl.multiple_of(HALF * i + QUARTER * y, QUARTER), QUARTER), own_g]
            else:
                spread[d][i].wait_recv()
                src = b_part.at[d - 1, i]
            turn.append(send(src, l_band.at[own_q, own_g], turned[d][i], slot + 2 * x + z % 2))
    grad.turn_z(1)
    grad.turn_x(1)
    grad.near_x()
    load_r.wait()
    load_sl.start()
    load_sr.start()
    r_swap.wait_recv()
    r_ring = Ring(along_y, y, pair(r_col), halves, share=True)
    grad.far_z()
    grad.far_x()
    for i in range(8):
        pltpu.make_async_copy(
            l_band.at[own_q, own_g], l_band.at[own_q, own_g], recv_sem.at[slot + i]
        ).wait()
    b_ring = Ring(along_y, y, band_refs, halves, share=True)
    grad.turn_rings()
    left.start_x(1)
    left.start_x(0)
    for ring in (r_ring, b_ring):
        ring.turn(1)
        ring.turn(-1)
    left.near_z()
    left.far_z()
    for ring in (r_ring, b_ring):
        ring.end(1)
        ring.end(-1)
    r_ring.got()

    base = (2 * y + h) * FULL

    def m_part(k):
        def refs(yy, part):
            lo, hi = spans[k]
            mid = (lo + hi) // 2
            lo, hi = {None: (lo, hi), 0: (lo, mid), 1: (mid, hi)}[part]
            return [m_col.at[pl.ds(pl.multiple_of((2 * yy + h) * FULL + lo, 16), hi - lo)]]

        return refs

    m_rings = []
    for k, (lo, hi) in enumerate(spans):
        grad.end(k)
        tile = nn(g_row[pl.ds(lo, hi - lo), :], r_col[...])
        m_col[pl.ds(pl.multiple_of(base + lo, 16), hi - lo), :] = tile.astype(jnp.bfloat16)
        m_rings.append(Ring(along_y, y, m_part(k), halves, share=True))

    left.turn_x(1)
    left.near_x()
    left.turn_x(0)

    band = [lanes(4 * z + xl), lanes(4 * z + 2 + xl)]

    @pl.loop(0, 4)
    def _(yy):
        other = g_row[:, lanes(4 * yy + 2 * (1 - h) + rep)]
        for i in range(2):
            q_out[yy, :, pl.ds(HALF * i, HALF)] = tn(other, g_row[:, band[i]]).astype(jnp.bfloat16)

    q_swap = send(q_out, q_in, mate)
    for ring in m_rings:
        ring.turn(1)
        ring.turn(-1)
    left.far_x()
    left.turn_rings()
    for ring in m_rings:
        ring.end(1)
        ring.end(-1)

    @pl.loop(0, 4)
    def _(yy):
        mine = g_row[:, lanes(4 * yy + 2 * h + rep)]
        for i in range(2):
            q_own[yy, :, pl.ds(HALF * i, HALF)] = tn(mine, g_row[:, band[i]])

    q_swap.wait_recv()

    @pl.loop(0, 4)
    def _(yy):
        total = q_own[yy] + q_in[yy].astype(jnp.float32)
        q_own[yy] = total
        s_out[yy] = total.astype(jnp.bfloat16)

    s_y = [send(s_out.at[(y + 4 + d) % 4], s_in.at[n], along_y(d)) for n, d in enumerate((1, -1, 2))]

    gain = (1.0 - decay_rate) / g_row.shape[1]
    load_sl.wait()
    load_sr.wait()
    b_ring.got()

    @pl.loop(0, 2)
    def _(i):
        part = pl.ds(pl.multiple_of(i * HALF, HALF), HALF)
        out_left[part, :] = decay_rate * state_l[part, :] + gain * nt(g_row[part, :], l_band[...])

    for ring in m_rings:
        ring.got()
    p_swap = []
    for k, (lo, hi) in enumerate(spans):
        part = pl.ds(lo, hi - lo)
        left.end(k)
        tile = nn(l_row[part, :], m_col[...])
        p_out[part, :] = tile.astype(jnp.bfloat16)
        p_swap.append(send(p_out.at[part, :], p_in.at[part, :], twin))
        out_pre[part, lanes(rep)] = tile

    for cp in s_y:
        cp.wait_recv()
    out_right[...] = decay_rate * state_r[...] + gain * (
        q_own[y] + s_in[0].astype(jnp.float32) + s_in[1].astype(jnp.float32) + s_in[2].astype(jnp.float32)
    )

    for k, (lo, hi) in enumerate(spans):
        part = pl.ds(lo, hi - lo)
        p_swap[k].wait_recv()
        out_pre[part, lanes(1 - rep)] = p_in[part, :].astype(jnp.float32)
    for cp in copies:
        cp.wait_send()
    assert len(copies) == N_COPIES, len(copies)


def shards(replica_deltas, weights, momentum, left_state, right_state, left_root, right_root):
    total = left_root.shape[0] * lax.axis_size("row")
    bf16, f32 = jnp.bfloat16, jnp.float32
    any_spec = pl.BlockSpec(memory_space=pl.ANY)
    vmem_spec = pl.BlockSpec(memory_space=pltpu.VMEM)
    update, new_left, new_right = pl.pallas_call(
        kernel,
        name="shampoo",
        out_shape=(
            jax.ShapeDtypeStruct((FULL, FULL), f32),
            jax.ShapeDtypeStruct((FULL, HALF), f32),
            jax.ShapeDtypeStruct((HALF, FULL), f32),
        ),
        in_specs=[any_spec] * 5,
        out_specs=[vmem_spec] * 3,
        scratch_shapes=[
            pltpu.VMEM((FULL, HALF), bf16),
            pltpu.VMEM((FULL, HALF), bf16),
            pltpu.VMEM((FULL, total), bf16),
            pltpu.VMEM((FULL, total), bf16),
            pltpu.VMEM((total, HALF), bf16),
            pltpu.VMEM((total, HALF), bf16),
            pltpu.VMEM((HALF, total), bf16),
            pltpu.VMEM((3, 2, QUARTER, HALF), bf16),
            pltpu.VMEM((4, HALF, FULL), bf16),
            pltpu.VMEM((4, HALF, FULL), f32),
            pltpu.VMEM((4, HALF, FULL), bf16),
            pltpu.VMEM((4, HALF, FULL), bf16),
            pltpu.VMEM((3, HALF, FULL), bf16),
            pltpu.VMEM((FULL, HALF), bf16),
            pltpu.VMEM((FULL, HALF), bf16),
            pltpu.VMEM((FULL, HALF), f32),
            pltpu.VMEM((HALF, FULL), f32),
            pltpu.SemaphoreType.DMA((5,)),
            pltpu.SemaphoreType.DMA((N_COPIES,)),
            pltpu.SemaphoreType.DMA((N_COPIES,)),
        ],
        compiler_params=pltpu.CompilerParams(
            collective_id=0, has_side_effects=True, vmem_limit_bytes=56 * 2**20
        ),
        cost_estimate=pl.CostEstimate(flops=8 * 2**30, bytes_accessed=4 * 2**20, transcendentals=0),
    )(replica_deltas[0], left_root, right_root, left_state, right_state)
    new_momentum = momentum_rate * momentum + update
    new_weights = weights - outer_rate * (momentum_rate * new_momentum + update)
    return (new_weights, new_momentum, new_left, new_right)


def solution(mesh):
    in_specs = (
        P("rep", "row", "col"),
        P("row", "col"),
        P("row", "col"),
        P("row", ("rep", "col")),
        P(("rep", "row"), "col"),
        P("row", ("rep", "col")),
        P(("rep", "row"), "col"),
    )
    out_specs = (
        P("row", "col"),
        P("row", "col"),
        P("row", ("rep", "col")),
        P(("rep", "row"), "col"),
    )
    return jax.shard_map(shards, mesh=mesh, in_specs=in_specs, out_specs=out_specs, check_vma=False)
```

```python
import functools

import jax
import jax.numpy as jnp
from jax import lax
from jax.experimental import pallas as pl
from jax.experimental.pallas import tpu as pltpu
from jax.sharding import PartitionSpec as P

decay_rate = 0.9
momentum_rate = 0.9
outer_rate = 0.7

MESH = pl.DeviceIdType.MESH
HALF = 256
FULL = 512
QUARTER = 64
SPLIT = 224
N_COPIES = 131


def lanes(chunk):
    return pl.ds(pl.multiple_of(chunk * HALF, HALF), HALF)


def rows_at(chunk, size):
    return pl.ds(pl.multiple_of(chunk * size, size), size)


def nn(a, b):
    return jnp.dot(a, b, preferred_element_type=jnp.float32)


def nt(a, b):
    return lax.dot_general(a, b, (((1,), (1,)), ((), ())), preferred_element_type=jnp.float32)


def tn(a, b):
    return lax.dot_general(a, b, (((0,), (0,)), ((), ())), preferred_element_type=jnp.float32)


def kernel(
    delta, left_root, right_root, left_state, right_state,
    out_pre, out_left, out_right,
    d_own, d_in, g_row, l_row, r_col, m_col, l_band,
    b_part, q_out, q_own, q_in, s_out, s_in, p_out, p_in, state_l, state_r,
    local_sem, send_sem, recv_sem,
):
    rep = lax.axis_index("rep")
    row = lax.axis_index("row")
    col = lax.axis_index("col")
    x, y, z, h = rep * 2 + col // 4, row // 2, col % 4, row % 2
    xl = col // 4

    def dev(xx, yy, zz, hh):
        return (xx // 2, yy * 2 + hh, (xx % 2) * 4 + zz)

    def along_x(d):
        return dev((x + 4 + d) % 4, y, z, h)

    def along_y(d):
        return dev(x, (y + 4 + d) % 4, z, h)

    def along_z(d):
        return dev(x, y, (z + 4 + d) % 4, h)

    mate = dev(x, y, z, 1 - h)
    twin = along_x(2)
    turned = [[dev((y + 4 - d) % 4, y, 2 * h + i, 1 - z // 2) for i in range(2)] for d in range(4)]
    turned_from = [dev(xx, y, 2 * (1 - h) + i, z // 2) for xx in range(4) for i in range(2)]

    copies = []

    def send(src, dst, device, slot=None):
        i = len(copies)
        cp = pltpu.make_async_remote_copy(
            src_ref=src, dst_ref=dst, send_sem=send_sem.at[i],
            recv_sem=recv_sem.at[i if slot is None else slot],
            device_id=device, device_id_type=MESH,
        )
        cp.start()
        copies.append(cp)
        return cp

    class Ring:
        def __init__(self, along, at, refs, onward, share=False):
            self.along, self.at, self.refs, self.onward, self.share = along, at, refs, onward, share
            self.shared = []
            self.first = {d: self.push(at, None, d) for d in (1, -1)}
            self.second = {}
            self.give(at, None)

        def push(self, i, part, d):
            return [send(r, r, self.along(d)) for r in self.refs(i, part)]

        def give(self, i, part):
            if self.share:
                self.shared += [send(r, r, mate) for r in self.refs(i, part)]

        def turn(self, d):
            for cp in self.first[d]:
                cp.wait_recv()
            i = (self.at + 4 - d) % 4
            if d in self.onward:
                self.second[d] = self.push(i, self.onward[d], d)
            self.give(i, None)

        def end(self, d):
            for cp in self.second[d]:
                cp.wait_recv()
            self.give((self.at + 2) % 4, self.onward[d])

        def got(self):
            for cp in self.shared:
                cp.wait_recv()

    halves = {1: 0, -1: 1}
    spans = ((0, SPLIT), (SPLIT, FULL))

    class Plane:
        def __init__(self, buf, spot, sign):
            self.buf, self.spot, self.sign = buf, spot, sign
            self.rings, self.z, self.x = [], [None, None], [None, None]

        def rows(self, span, part, xx, zz):
            lo, hi = span
            mid = (lo + hi) // 2
            lo, hi = {None: (lo, hi), 0: (lo, mid), 1: (mid, hi)}[part]
            return [self.buf.at[pl.ds(lo, hi - lo), lanes(self.spot(xx, zz))]]

        def start_z(self, k):
            refs = lambda i, part: self.rows(spans[k], part, x, i)
            self.z[k] = Ring(along_z, z, refs, {self.sign if k == 0 else -self.sign: None})

        def start_x(self, k):
            refs = lambda i, part: self.rows(spans[k], part, i, z)
            self.x[k] = Ring(along_x, x, refs, {self.sign if k == 1 else -self.sign: None})

        def on_x(self, zz):
            refs = lambda i, part: self.rows(spans[0], part, i, zz)
            self.rings.append(Ring(along_x, x, refs, halves))

        def on_z(self, xx):
            refs = lambda i, part: self.rows(spans[1], part, xx, i)
            self.rings.append(Ring(along_z, z, refs, halves))

        def turn_z(self, k):
            for d in (self.sign, -self.sign):
                self.z[k].turn(d)

        def turn_x(self, k):
            for d in (self.sign, -self.sign):
                self.x[k].turn(d)

        def near_z(self):
            self.on_x((z + 4 - self.sign) % 4)
            self.on_x((z + 4 + self.sign) % 4)

        def near_x(self):
            self.on_z((x + 4 - self.sign) % 4)
            self.on_z((x + 4 + self.sign) % 4)

        def far_z(self):
            self.z[0].end(self.sign)
            self.on_x((z + 2) % 4)

        def far_x(self):
            self.x[1].end(self.sign)
            self.on_z((x + 2) % 4)

        def turn_rings(self):
            for ring in self.rings:
                ring.turn(1)
                ring.turn(-1)

        def end(self, k):
            (self.x, self.z)[k][k].end(-self.sign)
            for ring in self.rings:
                if ring.along is (along_x, along_z)[k]:
                    ring.end(1)
                    ring.end(-1)

    own_g = lanes(4 * z + x)
    own_l = lanes(4 * x + z)
    own_r = rows_at(4 * y + 2 * h + rep, HALF)
    load_l = pltpu.make_async_copy(left_root, l_row.at[:, own_l], local_sem.at[0])
    load_d = pltpu.make_async_copy(delta.at[:, lanes(rep)], d_own, local_sem.at[1])
    load_r = pltpu.make_async_copy(right_root.at[:, lanes(rep)], r_col.at[own_r], local_sem.at[2])
    load_d.start()
    load_l.start()
    load_r.start()
    load_sl = pltpu.make_async_copy(left_state, state_l, local_sem.at[3])
    load_sr = pltpu.make_async_copy(right_state, state_r, local_sem.at[4])

    barrier = pltpu.get_barrier_semaphore()
    partners = [f(d) for f in (along_x, along_y, along_z) for d in (1, -1)]
    partners += [twin, mate, along_y(2)] + sum(turned, []) + turned_from
    for partner in partners:
        pl.semaphore_signal(barrier, inc=1, device_id=partner, device_id_type=MESH)
    pl.semaphore_wait(barrier, len(partners))

    d_swap = []
    for lo, hi in spans:
        part = pl.ds(lo, hi - lo)
        d_swap.append(send(delta.at[part, lanes(1 - rep)], d_in.at[part, :], twin))
    load_l.wait()
    left = Plane(l_row, lambda xx, zz: 4 * xx + zz, -1)
    left.start_z(0)
    left.start_z(1)

    load_d.wait()
    grad = Plane(g_row, lambda xx, zz: 4 * zz + xx, 1)
    for k, (lo, hi) in enumerate(spans):
        part = pl.ds(lo, hi - lo)
        d_swap[k].wait_recv()
        g_row[part, own_g] = (
            (d_own[part, :].astype(jnp.float32) + d_in[part, :].astype(jnp.float32)) * 0.5
        ).astype(jnp.bfloat16)
        grad.start_z(k)
        grad.start_x(k)
    spread = {
        d: [
            send(
                g_row.at[pl.ds(pl.multiple_of(HALF * i + QUARTER * ((y + d) % 4), QUARTER), QUARTER), own_g],
                b_part.at[d - 1, i], along_y(d),
            )
            for i in range(2)
        ]
        for d in (1, 3, 2)
    }
    r_swap = send(right_root.at[:, lanes(1 - rep)], r_col.at[own_r], twin)
    left.turn_z(0)
    left.turn_z(1)

    def pair(buf):
        def refs(yy, part):
            base, size = (2 * yy + h) * FULL, FULL
            if part is not None:
                base, size = base + part * HALF, HALF
            return [buf.at[pl.ds(pl.multiple_of(base, HALF), size)]]

        return refs

    side = pl.ds(pl.multiple_of((1 - h) * 8 * HALF, HALF), 8 * HALF)

    def band_refs(yy, part):
        lo, size = QUARTER * yy, QUARTER
        if part is not None:
            lo, size = lo + part * (QUARTER // 2), QUARTER // 2
        return [l_band.at[pl.ds(pl.multiple_of(lo, QUARTER // 2), size), side]]

    grad.turn_z(0)
    grad.near_z()
    grad.turn_x(0)
    turn = []
    slot = len(copies)
    own_q = pl.ds(pl.multiple_of(QUARTER * y, QUARTER), QUARTER)
    for d in (0, 1, 3, 2):
        for i in range(2):
            if d == 0:
                src = g_row.at[pl.ds(pl.multiple_of(HALF * i + QUARTER * y, QUARTER), QUARTER), own_g]
            else:
                spread[d][i].wait_recv()
                src = b_part.at[d - 1, i]
            turn.append(send(src, l_band.at[own_q, own_g], turned[d][i], slot + 2 * x + z % 2))
    grad.turn_z(1)
    grad.turn_x(1)
    grad.near_x()
    load_r.wait()
    load_sl.start()
    load_sr.start()
    r_swap.wait_recv()
    r_ring = Ring(along_y, y, pair(r_col), halves, share=True)
    grad.far_z()
    grad.far_x()
    for i in range(8):
        pltpu.make_async_copy(
            l_band.at[own_q, own_g], l_band.at[own_q, own_g], recv_sem.at[slot + i]
        ).wait()
    b_ring = Ring(along_y, y, band_refs, halves, share=True)
    grad.turn_rings()
    left.start_x(1)
    left.start_x(0)
    for ring in (r_ring, b_ring):
        ring.turn(1)
        ring.turn(-1)
    left.near_z()
    left.far_z()
    for ring in (r_ring, b_ring):
        ring.end(1)
        ring.end(-1)
    r_ring.got()

    base = (2 * y + h) * FULL

    def m_part(k):
        def refs(yy, part):
            lo, hi = spans[k]
            mid = (lo + hi) // 2
            lo, hi = {None: (lo, hi), 0: (lo, mid), 1: (mid, hi)}[part]
            return [m_col.at[pl.ds(pl.multiple_of((2 * yy + h) * FULL + lo, 16), hi - lo)]]

        return refs

    left.turn_x(1)
    left.near_x()
    left.turn_x(0)
    m_rings = []
    for k, (lo, hi) in enumerate(spans):
        grad.end(k)
        tile = nn(g_row[pl.ds(lo, hi - lo), :], r_col[...])
        m_col[pl.ds(pl.multiple_of(base + lo, 16), hi - lo), :] = tile.astype(jnp.bfloat16)
        m_rings.append(Ring(along_y, y, m_part(k), halves, share=True))


    band = [lanes(4 * z + xl), lanes(4 * z + 2 + xl)]

    @pl.loop(0, 4)
    def _(yy):
        other = g_row[:, lanes(4 * yy + 2 * (1 - h) + rep)]
        for i in range(2):
            q_out[yy, :, pl.ds(HALF * i, HALF)] = tn(other, g_row[:, band[i]]).astype(jnp.bfloat16)

    q_swap = send(q_out, q_in, mate)
    for ring in m_rings:
        ring.turn(1)
        ring.turn(-1)
    @pl.loop(0, 4)
    def _(yy):
        mine = g_row[:, lanes(4 * yy + 2 * h + rep)]
        for i in range(2):
            q_own[yy, :, pl.ds(HALF * i, HALF)] = tn(mine, g_row[:, band[i]])

    left.far_x()
    left.turn_rings()
    for ring in m_rings:
        ring.end(1)
        ring.end(-1)

    q_swap.wait_recv()

    @pl.loop(0, 4)
    def _(yy):
        total = q_own[yy] + q_in[yy].astype(jnp.float32)
        q_own[yy] = total
        s_out[yy] = total.astype(jnp.bfloat16)

    s_y = [send(s_out.at[(y + 4 + d) % 4], s_in.at[n], along_y(d)) for n, d in enumerate((1, -1, 2))]

    for ring in m_rings:
        ring.got()
    p_swap = []
    for k, (lo, hi) in enumerate(spans):
        part = pl.ds(lo, hi - lo)
        left.end(k)
        tile = nn(l_row[part, :], m_col[...])
        p_out[part, :] = tile.astype(jnp.bfloat16)
        p_swap.append(send(p_out.at[part, :], p_in.at[part, :], twin))
        out_pre[part, lanes(rep)] = tile

    gain = (1.0 - decay_rate) / g_row.shape[1]
    load_sl.wait()
    load_sr.wait()
    b_ring.got()

    @pl.loop(0, 2)
    def _(i):
        part = pl.ds(pl.multiple_of(i * HALF, HALF), HALF)
        out_left[part, :] = decay_rate * state_l[part, :] + gain * nt(g_row[part, :], l_band[...])

    for cp in s_y:
        cp.wait_recv()
    out_right[...] = decay_rate * state_r[...] + gain * (
        q_own[y] + s_in[0].astype(jnp.float32) + s_in[1].astype(jnp.float32) + s_in[2].astype(jnp.float32)
    )

    for k, (lo, hi) in enumerate(spans):
        part = pl.ds(lo, hi - lo)
        p_swap[k].wait_recv()
        out_pre[part, lanes(1 - rep)] = p_in[part, :].astype(jnp.float32)
    for cp in copies:
        cp.wait_send()
    assert len(copies) == N_COPIES, len(copies)


def shards(replica_deltas, weights, momentum, left_state, right_state, left_root, right_root):
    total = left_root.shape[0] * lax.axis_size("row")
    bf16, f32 = jnp.bfloat16, jnp.float32
    any_spec = pl.BlockSpec(memory_space=pl.ANY)
    vmem_spec = pl.BlockSpec(memory_space=pltpu.VMEM)
    update, new_left, new_right = pl.pallas_call(
        kernel,
        name="shampoo",
        out_shape=(
            jax.ShapeDtypeStruct((FULL, FULL), f32),
            jax.ShapeDtypeStruct((FULL, HALF), f32),
            jax.ShapeDtypeStruct((HALF, FULL), f32),
        ),
        in_specs=[any_spec] * 5,
        out_specs=[vmem_spec] * 3,
        scratch_shapes=[
            pltpu.VMEM((FULL, HALF), bf16),
            pltpu.VMEM((FULL, HALF), bf16),
            pltpu.VMEM((FULL, total), bf16),
            pltpu.VMEM((FULL, total), bf16),
            pltpu.VMEM((total, HALF), bf16),
            pltpu.VMEM((total, HALF), bf16),
            pltpu.VMEM((HALF, total), bf16),
            pltpu.VMEM((3, 2, QUARTER, HALF), bf16),
            pltpu.VMEM((4, HALF, FULL), bf16),
            pltpu.VMEM((4, HALF, FULL), f32),
            pltpu.VMEM((4, HALF, FULL), bf16),
            pltpu.VMEM((4, HALF, FULL), bf16),
            pltpu.VMEM((3, HALF, FULL), bf16),
            pltpu.VMEM((FULL, HALF), bf16),
            pltpu.VMEM((FULL, HALF), bf16),
            pltpu.VMEM((FULL, HALF), f32),
            pltpu.VMEM((HALF, FULL), f32),
            pltpu.SemaphoreType.DMA((5,)),
            pltpu.SemaphoreType.DMA((N_COPIES,)),
            pltpu.SemaphoreType.DMA((N_COPIES,)),
        ],
        compiler_params=pltpu.CompilerParams(
            collective_id=0, has_side_effects=True, vmem_limit_bytes=56 * 2**20
        ),
        cost_estimate=pl.CostEstimate(flops=8 * 2**30, bytes_accessed=4 * 2**20, transcendentals=0),
    )(replica_deltas[0], left_root, right_root, left_state, right_state)
    new_momentum = momentum_rate * momentum + update
    new_weights = weights - outer_rate * (momentum_rate * new_momentum + update)
    return (new_weights, new_momentum, new_left, new_right)


def solution(mesh):
    in_specs = (
        P("rep", "row", "col"),
        P("row", "col"),
        P("row", "col"),
        P("row", ("rep", "col")),
        P(("rep", "row"), "col"),
        P("row", ("rep", "col")),
        P(("rep", "row"), "col"),
    )
    out_specs = (
        P("row", "col"),
        P("row", "col"),
        P("row", ("rep", "col")),
        P(("rep", "row"), "col"),
    )
    return jax.shard_map(shards, mesh=mesh, in_specs=in_specs, out_specs=out_specs, check_vma=False)
```

```python
import functools

import jax
import jax.numpy as jnp
from jax import lax
from jax.experimental import pallas as pl
from jax.experimental.pallas import tpu as pltpu
from jax.sharding import PartitionSpec as P

decay_rate = 0.9
momentum_rate = 0.9
outer_rate = 0.7

MESH = pl.DeviceIdType.MESH
HALF = 256
FULL = 512
QUARTER = 64
SPLIT = 224
N_COPIES = 131


def lanes(chunk):
    return pl.ds(pl.multiple_of(chunk * HALF, HALF), HALF)


def rows_at(chunk, size):
    return pl.ds(pl.multiple_of(chunk * size, size), size)


def nn(a, b):
    return jnp.dot(a, b, preferred_element_type=jnp.float32)


def nt(a, b):
    return lax.dot_general(a, b, (((1,), (1,)), ((), ())), preferred_element_type=jnp.float32)


def tn(a, b):
    return lax.dot_general(a, b, (((0,), (0,)), ((), ())), preferred_element_type=jnp.float32)


def kernel(
    delta, left_root, right_root, left_state, right_state,
    out_pre, out_left, out_right,
    d_own, d_in, g_row, l_row, r_col, m_col, l_band,
    b_part, q_out, q_own, q_in, s_out, s_in, p_out, p_in, state_l, state_r,
    local_sem, send_sem, recv_sem,
):
    rep = lax.axis_index("rep")
    row = lax.axis_index("row")
    col = lax.axis_index("col")
    x, y, z, h = rep * 2 + col // 4, row // 2, col % 4, row % 2
    xl = col // 4

    def dev(xx, yy, zz, hh):
        return (xx // 2, yy * 2 + hh, (xx % 2) * 4 + zz)

    def along_x(d):
        return dev((x + 4 + d) % 4, y, z, h)

    def along_y(d):
        return dev(x, (y + 4 + d) % 4, z, h)

    def along_z(d):
        return dev(x, y, (z + 4 + d) % 4, h)

    mate = dev(x, y, z, 1 - h)
    twin = along_x(2)
    turned = [[dev((y + 4 - d) % 4, y, 2 * h + i, 1 - z // 2) for i in range(2)] for d in range(4)]
    turned_from = [dev(xx, y, 2 * (1 - h) + i, z // 2) for xx in range(4) for i in range(2)]

    copies = []

    def send(src, dst, device, slot=None):
        i = len(copies)
        cp = pltpu.make_async_remote_copy(
            src_ref=src, dst_ref=dst, send_sem=send_sem.at[i],
            recv_sem=recv_sem.at[i if slot is None else slot],
            device_id=device, device_id_type=MESH,
        )
        cp.start()
        copies.append(cp)
        return cp

    class Ring:
        def __init__(self, along, at, refs, onward, share=False):
            self.along, self.at, self.refs, self.onward, self.share = along, at, refs, onward, share
            self.shared = []
            self.first = {d: self.push(at, None, d) for d in (1, -1)}
            self.second = {}
            self.give(at, None)

        def push(self, i, part, d):
            return [send(r, r, self.along(d)) for r in self.refs(i, part)]

        def give(self, i, part):
            if self.share:
                self.shared += [send(r, r, mate) for r in self.refs(i, part)]

        def turn(self, d):
            for cp in self.first[d]:
                cp.wait_recv()
            i = (self.at + 4 - d) % 4
            if d in self.onward:
                self.second[d] = self.push(i, self.onward[d], d)
            self.give(i, None)

        def end(self, d):
            for cp in self.second[d]:
                cp.wait_recv()
            self.give((self.at + 2) % 4, self.onward[d])

        def got(self):
            for cp in self.shared:
                cp.wait_recv()

    halves = {1: 0, -1: 1}
    spans = ((0, SPLIT), (SPLIT, FULL))

    class Plane:
        def __init__(self, buf, spot, sign):
            self.buf, self.spot, self.sign = buf, spot, sign
            self.rings, self.z, self.x = [], [None, None], [None, None]

        def rows(self, span, part, xx, zz):
            lo, hi = span
            mid = (lo + hi) // 2
            lo, hi = {None: (lo, hi), 0: (lo, mid), 1: (mid, hi)}[part]
            return [self.buf.at[pl.ds(lo, hi - lo), lanes(self.spot(xx, zz))]]

        def start_z(self, k):
            refs = lambda i, part: self.rows(spans[k], part, x, i)
            self.z[k] = Ring(along_z, z, refs, {self.sign if k == 0 else -self.sign: None})

        def start_x(self, k):
            refs = lambda i, part: self.rows(spans[k], part, i, z)
            self.x[k] = Ring(along_x, x, refs, {self.sign if k == 1 else -self.sign: None})

        def on_x(self, zz):
            refs = lambda i, part: self.rows(spans[0], part, i, zz)
            self.rings.append(Ring(along_x, x, refs, halves))

        def on_z(self, xx):
            refs = lambda i, part: self.rows(spans[1], part, xx, i)
            self.rings.append(Ring(along_z, z, refs, halves))

        def turn_z(self, k):
            for d in (self.sign, -self.sign):
                self.z[k].turn(d)

        def turn_x(self, k):
            for d in (self.sign, -self.sign):
                self.x[k].turn(d)

        def near_z(self):
            self.on_x((z + 4 - self.sign) % 4)
            self.on_x((z + 4 + self.sign) % 4)

        def near_x(self):
            self.on_z((x + 4 - self.sign) % 4)
            self.on_z((x + 4 + self.sign) % 4)

        def far_z(self):
            self.z[0].end(self.sign)
            self.on_x((z + 2) % 4)

        def far_x(self):
            self.x[1].end(self.sign)
            self.on_z((x + 2) % 4)

        def turn_rings(self):
            for ring in self.rings:
                ring.turn(1)
                ring.turn(-1)

        def end(self, k):
            (self.x, self.z)[k][k].end(-self.sign)
            for ring in self.rings:
                if ring.along is (along_x, along_z)[k]:
                    ring.end(1)
                    ring.end(-1)

    own_g = lanes(4 * z + x)
    own_l = lanes(4 * x + z)
    own_r = rows_at(4 * y + 2 * h + rep, HALF)
    load_l = pltpu.make_async_copy(left_root, l_row.at[:, own_l], local_sem.at[0])
    load_d = pltpu.make_async_copy(delta.at[:, lanes(rep)], d_own, local_sem.at[1])
    load_r = pltpu.make_async_copy(right_root.at[:, lanes(rep)], r_col.at[own_r], local_sem.at[2])
    load_d.start()
    load_l.start()
    load_r.start()
    load_sl = pltpu.make_async_copy(left_state, state_l, local_sem.at[3])
    load_sr = pltpu.make_async_copy(right_state, state_r, local_sem.at[4])

    barrier = pltpu.get_barrier_semaphore()
    partners = [f(d) for f in (along_x, along_y, along_z) for d in (1, -1)]
    partners += [twin, mate, along_y(2)] + sum(turned, []) + turned_from
    for partner in partners:
        pl.semaphore_signal(barrier, inc=1, device_id=partner, device_id_type=MESH)
    pl.semaphore_wait(barrier, len(partners))

    d_swap = []
    for lo, hi in spans:
        part = pl.ds(lo, hi - lo)
        d_swap.append(send(delta.at[part, lanes(1 - rep)], d_in.at[part, :], twin))
    load_l.wait()
    left = Plane(l_row, lambda xx, zz: 4 * xx + zz, -1)
    left.start_z(0)
    left.start_z(1)

    load_d.wait()
    grad = Plane(g_row, lambda xx, zz: 4 * zz + xx, 1)
    for k, (lo, hi) in enumerate(spans):
        part = pl.ds(lo, hi - lo)
        d_swap[k].wait_recv()
        g_row[part, own_g] = (
            (d_own[part, :].astype(jnp.float32) + d_in[part, :].astype(jnp.float32)) * 0.5
        ).astype(jnp.bfloat16)
        grad.start_z(k)
        grad.start_x(k)
    r_swap = send(right_root.at[:, lanes(1 - rep)], r_col.at[own_r], twin)
    spread = {
        d: [
            send(
                g_row.at[pl.ds(pl.multiple_of(HALF * i + QUARTER * ((y + d) % 4), QUARTER), QUARTER), own_g],
                b_part.at[d - 1, i], along_y(d),
            )
            for i in range(2)
        ]
        for d in (1, 3, 2)
    }
    left.turn_z(0)
    left.turn_z(1)

    def pair(buf):
        def refs(yy, part):
            base, size = (2 * yy + h) * FULL, FULL
            if part is not None:
                base, size = base + part * HALF, HALF
            return [buf.at[pl.ds(pl.multiple_of(base, HALF), size)]]

        return refs

    side = pl.ds(pl.multiple_of((1 - h) * 8 * HALF, HALF), 8 * HALF)

    def band_refs(yy, part):
        lo, size = QUARTER * yy, QUARTER
        if part is not None:
            lo, size = lo + part * (QUARTER // 2), QUARTER // 2
        return [l_band.at[pl.ds(pl.multiple_of(lo, QUARTER // 2), size), side]]

    grad.turn_z(0)
    grad.near_z()
    grad.turn_x(0)
    turn = []
    slot = len(copies)
    own_q = pl.ds(pl.multiple_of(QUARTER * y, QUARTER), QUARTER)
    for d in (0, 1, 3, 2):
        for i in range(2):
            if d == 0:
                src = g_row.at[pl.ds(pl.multiple_of(HALF * i + QUARTER * y, QUARTER), QUARTER), own_g]
            else:
                spread[d][i].wait_recv()
                src = b_part.at[d - 1, i]
            turn.append(send(src, l_band.at[own_q, own_g], turned[d][i], slot + 2 * x + z % 2))
    grad.turn_z(1)
    grad.turn_x(1)
    grad.near_x()
    load_r.wait()
    load_sl.start()
    load_sr.start()
    r_swap.wait_recv()
    r_ring = Ring(along_y, y, pair(r_col), halves, share=True)
    grad.far_z()
    grad.far_x()
    for i in range(8):
        pltpu.make_async_copy(
            l_band.at[own_q, own_g], l_band.at[own_q, own_g], recv_sem.at[slot + i]
        ).wait()
    b_ring = Ring(along_y, y, band_refs, halves, share=True)
    grad.turn_rings()
    left.start_x(1)
    left.start_x(0)
    for ring in (r_ring, b_ring):
        ring.turn(1)
        ring.turn(-1)
    left.near_z()
    left.far_z()
    for ring in (r_ring, b_ring):
        ring.end(1)
        ring.end(-1)
    r_ring.got()

    base = (2 * y + h) * FULL

    def m_part(k):
        def refs(yy, part):
            lo, hi = spans[k]
            mid = (lo + hi) // 2
            lo, hi = {None: (lo, hi), 0: (lo, mid), 1: (mid, hi)}[part]
            return [m_col.at[pl.ds(pl.multiple_of((2 * yy + h) * FULL + lo, 16), hi - lo)]]

        return refs

    left.turn_x(1)
    left.near_x()
    left.turn_x(0)
    m_rings = []
    for k, (lo, hi) in enumerate(spans):
        grad.end(k)
        tile = nn(g_row[pl.ds(lo, hi - lo), :], r_col[...])
        m_col[pl.ds(pl.multiple_of(base + lo, 16), hi - lo), :] = tile.astype(jnp.bfloat16)
        m_rings.append(Ring(along_y, y, m_part(k), halves, share=True))


    band = [lanes(4 * z + xl), lanes(4 * z + 2 + xl)]

    @pl.loop(0, 4)
    def _(yy):
        other = g_row[:, lanes(4 * yy + 2 * (1 - h) + rep)]
        for i in range(2):
            q_out[yy, :, pl.ds(HALF * i, HALF)] = tn(other, g_row[:, band[i]]).astype(jnp.bfloat16)

    q_swap = send(q_out, q_in, mate)
    for ring in m_rings:
        ring.turn(1)
        ring.turn(-1)
    @pl.loop(0, 4)
    def _(yy):
        mine = g_row[:, lanes(4 * yy + 2 * h + rep)]
        for i in range(2):
            q_own[yy, :, pl.ds(HALF * i, HALF)] = tn(mine, g_row[:, band[i]])

    left.far_x()
    left.turn_rings()
    for ring in m_rings:
        ring.end(1)
        ring.end(-1)

    q_swap.wait_recv()

    @pl.loop(0, 4)
    def _(yy):
        total = q_own[yy] + q_in[yy].astype(jnp.float32)
        q_own[yy] = total
        s_out[yy] = total.astype(jnp.bfloat16)

    s_y = [send(s_out.at[(y + 4 + d) % 4], s_in.at[n], along_y(d)) for n, d in enumerate((1, -1, 2))]

    for ring in m_rings:
        ring.got()
    p_swap = []
    for k, (lo, hi) in enumerate(spans):
        part = pl.ds(lo, hi - lo)
        left.end(k)
        tile = nn(l_row[part, :], m_col[...])
        p_out[part, :] = tile.astype(jnp.bfloat16)
        p_swap.append(send(p_out.at[part, :], p_in.at[part, :], twin))
        out_pre[part, lanes(rep)] = tile

    gain = (1.0 - decay_rate) / g_row.shape[1]
    load_sl.wait()
    load_sr.wait()
    b_ring.got()

    @pl.loop(0, 2)
    def _(i):
        part = pl.ds(pl.multiple_of(i * HALF, HALF), HALF)
        out_left[part, :] = decay_rate * state_l[part, :] + gain * nt(g_row[part, :], l_band[...])

    for cp in s_y:
        cp.wait_recv()
    out_right[...] = decay_rate * state_r[...] + gain * (
        q_own[y] + s_in[0].astype(jnp.float32) + s_in[1].astype(jnp.float32) + s_in[2].astype(jnp.float32)
    )

    for k, (lo, hi) in enumerate(spans):
        part = pl.ds(lo, hi - lo)
        p_swap[k].wait_recv()
        out_pre[part, lanes(1 - rep)] = p_in[part, :].astype(jnp.float32)
    for cp in copies:
        cp.wait_send()
    assert len(copies) == N_COPIES, len(copies)


def shards(replica_deltas, weights, momentum, left_state, right_state, left_root, right_root):
    total = left_root.shape[0] * lax.axis_size("row")
    bf16, f32 = jnp.bfloat16, jnp.float32
    any_spec = pl.BlockSpec(memory_space=pl.ANY)
    vmem_spec = pl.BlockSpec(memory_space=pltpu.VMEM)
    update, new_left, new_right = pl.pallas_call(
        kernel,
        name="shampoo",
        out_shape=(
            jax.ShapeDtypeStruct((FULL, FULL), f32),
            jax.ShapeDtypeStruct((FULL, HALF), f32),
            jax.ShapeDtypeStruct((HALF, FULL), f32),
        ),
        in_specs=[any_spec] * 5,
        out_specs=[vmem_spec] * 3,
        scratch_shapes=[
            pltpu.VMEM((FULL, HALF), bf16),
            pltpu.VMEM((FULL, HALF), bf16),
            pltpu.VMEM((FULL, total), bf16),
            pltpu.VMEM((FULL, total), bf16),
            pltpu.VMEM((total, HALF), bf16),
            pltpu.VMEM((total, HALF), bf16),
            pltpu.VMEM((HALF, total), bf16),
            pltpu.VMEM((3, 2, QUARTER, HALF), bf16),
            pltpu.VMEM((4, HALF, FULL), bf16),
            pltpu.VMEM((4, HALF, FULL), f32),
            pltpu.VMEM((4, HALF, FULL), bf16),
            pltpu.VMEM((4, HALF, FULL), bf16),
            pltpu.VMEM((3, HALF, FULL), bf16),
            pltpu.VMEM((FULL, HALF), bf16),
            pltpu.VMEM((FULL, HALF), bf16),
            pltpu.VMEM((FULL, HALF), f32),
            pltpu.VMEM((HALF, FULL), f32),
            pltpu.SemaphoreType.DMA((5,)),
            pltpu.SemaphoreType.DMA((N_COPIES,)),
            pltpu.SemaphoreType.DMA((N_COPIES,)),
        ],
        compiler_params=pltpu.CompilerParams(
            collective_id=0, has_side_effects=True, vmem_limit_bytes=56 * 2**20
        ),
        cost_estimate=pl.CostEstimate(flops=8 * 2**30, bytes_accessed=4 * 2**20, transcendentals=0),
    )(replica_deltas[0], left_root, right_root, left_state, right_state)
    new_momentum = momentum_rate * momentum + update
    new_weights = weights - outer_rate * (momentum_rate * new_momentum + update)
    return (new_weights, new_momentum, new_left, new_right)


def solution(mesh):
    in_specs = (
        P("rep", "row", "col"),
        P("row", "col"),
        P("row", "col"),
        P("row", ("rep", "col")),
        P(("rep", "row"), "col"),
        P("row", ("rep", "col")),
        P(("rep", "row"), "col"),
    )
    out_specs = (
        P("row", "col"),
        P("row", "col"),
        P("row", ("rep", "col")),
        P(("rep", "row"), "col"),
    )
    return jax.shard_map(shards, mesh=mesh, in_specs=in_specs, out_specs=out_specs, check_vma=False)
```
